128 devices in a mesh: coarse: 4 (over z_hi, core), leaf: 32 (over x, y, z_lo).
Axes of the slice: x: 4, y: 4, z: 4 (z_hi: 2, z_lo: 2; z = z_hi * 2 + z_lo), core: 2. Of those that a mesh axis runs over, the one named last changes fastest.
Arguments:
- densities: bfloat16 [65536, 128], P(('coarse', 'leaf')), may hold values from -6 to 6
- cotangents: bfloat16 [65536, 128], P(('coarse', 'leaf')), may hold values from -6 to 6
- far_list: int32 [16, 65536], P(None, ('coarse', 'leaf')), may hold values from -1 to 256, as said below
- near_list: int32 [27, 65536], P(None, ('coarse', 'leaf')), may hold values from -1 to 256, as said below
- coarse_list: int32 [16, 16], replicated, may hold values from -1 to 15, as said below
- to_moments: bfloat16 [128, 256], replicated, may hold values from -0.5 to 0.5
- merge_moments: bfloat16 [8, 256, 256], replicated, may hold values from -0.125 to 0.125
- far_translate: bfloat16 [16, 256, 256], replicated, may hold values from -0.09375 to 0.09375
- local_split: bfloat16 [256, 8, 256], replicated, may hold values from -0.375 to 0.375
- to_values: bfloat16 [256, 128], replicated, may hold values from -0.375 to 0.375
- near_blocks: bfloat16 [27, 128, 128], replicated, may hold values from -0.109375 to 0.109375
Outputs:
- potential: float32 [65536, 128], P(('coarse', 'leaf'))
- gradient: float32 [65536, 128], P(('coarse', 'leaf'))
The draws below stay inside these ranges and needn't reach their ends.
Inputs may be any that keep to these rules, and one draw needn't show every extreme that they name: `far_list`: -1 marks an empty slot; any other entry e of box b names the leaf box b + e - 128, which exists. `near_list`: -1 marks an empty slot; any other entry e of box b names the leaf box b + e - 128, which exists. `coarse_list`: -1 marks an empty slot; any other entry is a box of the coarse level.
All inputs are finite; a program needn't handle non-finite values.
Results may differ from the reference program's by a relative error of at most 0.018.
Values may be sent and summed in bfloat16 or wider, within the bound.
No kernel may reach another device: no remote copies, remote signals or barrier semaphores. Data moves between devices by JAX's collectives and lax.ppermute only.
A program may use at most 128 MiB of HBM per device.

```python
import jax
import jax.numpy as jnp

NP = 128
K = 256
NLIST = 16
NNEAR = 27
HW = 128
NL = 65536
NC4 = 16


def window_entries(key, slots, blank_odds):
    offset_key, retain_key = jax.random.split(key)
    positions = jnp.arange(NL, dtype=jnp.int32)[None, :]
    offsets = jax.random.randint(offset_key, (slots, NL), -HW, HW + 1, dtype=jnp.int32)
    retained = jax.random.randint(retain_key, (slots, NL), 0, blank_odds, dtype=jnp.int32) != 0
    sources = positions + offsets
    inside = (sources >= 0) & (sources < NL) & retained
    matrix_entries = jnp.where(inside, offsets + HW, -1)
    matrix_entries = matrix_entries.at[0, 0].set(2 * HW)
    matrix_entries = matrix_entries.at[1, NL - 1].set(0)
    return matrix_entries.astype(jnp.int32)


def draw_far_list(key, part):
    key = jax.random.fold_in(key, 11)
    return window_entries(key, NLIST, 4)


def draw_near_list(key, part):
    key = jax.random.fold_in(key, 12)
    return window_entries(key, NNEAR, 8)


def draw_coarse_list(key, part):
    key = jax.random.fold_in(key, 13)
    source_key, retain_key = jax.random.split(key)
    sources = jax.random.randint(source_key, (NLIST, NC4), 0, NC4, dtype=jnp.int32)
    retained = jax.random.randint(retain_key, (NLIST, NC4), 0, 4, dtype=jnp.int32) != 0
    matrix_entries = jnp.where(retained, sources, -1)
    matrix_entries = matrix_entries.at[0, 0].set(NC4 - 1)
    matrix_entries = matrix_entries.at[1, 0].set(-1)
    return matrix_entries.astype(jnp.int32)


def block_scale(own_key, shape, cuts, least, largest):
    level = 1.0
    for position, parts in cuts:
        heights = jax.random.uniform(jax.random.fold_in(jax.random.fold_in(own_key, 6), position), (parts,), jnp.float32, least / len(cuts), largest / len(cuts))
        level = level * jnp.repeat(jnp.exp(heights), shape[position] // parts).reshape((-1,) + (1,) * (len(shape) - 1 - position))
    return level


def scatter_about(own_key, extent, scale, bound, shards=(), held_as=jnp.bfloat16):
    loudness = block_scale(own_key, extent, shards, -0.22, 0.18) if shards else 1.0
    entries = jax.random.normal(own_key, extent, jnp.float32) * scale * loudness
    return jnp.minimum(jnp.maximum(entries, -bound), bound).astype(held_as)


def setup_inputs(seed: int = 0) -> dict:
    seeds = jax.random.split(jax.random.key(seed), 12)
    densities = scatter_about(seeds[0], (NL, NP), 1.0, 6.0, ((0, 128),))
    cotangents = scatter_about(seeds[1], (NL, NP), 1.0, 6.0, ((0, 128),))
    far_list = draw_far_list(jax.random.fold_in(seeds[11], 71), 0)
    near_list = draw_near_list(jax.random.fold_in(seeds[11], 71), 0)
    coarse_list = draw_coarse_list(jax.random.fold_in(seeds[11], 71), 0)
    to_moments = scatter_about(seeds[5], (NP, K), NP ** -0.5, 0.5)
    merge_moments = scatter_about(seeds[6], (8, K, K), (8 * K) ** -0.5, 0.125)
    far_translate = scatter_about(seeds[7], (NLIST, K, K), (NLIST * K) ** -0.5, 0.09375)
    local_split = scatter_about(seeds[8], (K, 8, K), K ** -0.5, 0.375)
    to_values = scatter_about(seeds[9], (K, NP), K ** -0.5, 0.375)
    near_blocks = scatter_about(seeds[10], (NNEAR, NP, NP), (NNEAR * NP) ** -0.5, 0.109375)
    return {"densities": densities, "cotangents": cotangents, "far_list": far_list, "near_list": near_list, "coarse_list": coarse_list, "to_moments": to_moments, "merge_moments": merge_moments, "far_translate": far_translate, "local_split": local_split, "to_values": to_values, "near_blocks": near_blocks}


def absolute_entries(lists):
    positions = jnp.arange(lists.shape[1], dtype=jnp.int32)[None, :]
    return jnp.where(lists >= 0, positions + lists - HW, -1).astype(jnp.int32)


def gather_rows(source_row_ids, matrix_entries):
    present = (matrix_entries >= 0)[:, None]
    picked = jnp.take(source_row_ids, jnp.maximum(matrix_entries, 0), axis=0)
    return jnp.where(present, picked, jnp.zeros_like(picked))


def listed_sum(source_row_ids, lists, translation_operators):
    running_totals = jnp.zeros((lists.shape[1], translation_operators.shape[2]), jnp.float32)
    for position_index in range(lists.shape[0]):
        picked = gather_rows(source_row_ids, lists[position_index])
        running_totals = running_totals + jnp.dot(picked, translation_operators[position_index], preferred_element_type=jnp.float32)
    return running_totals


def listed_scatter(source_row_ids, lists, translation_operators, target_count):
    running_totals = jnp.zeros((target_count, translation_operators.shape[1]), jnp.float32)
    for position_index in range(lists.shape[0]):
        matrix_entries = lists[position_index]
        summand_terms = jnp.dot(source_row_ids, translation_operators[position_index].T, preferred_element_type=jnp.float32)
        summand_terms = jnp.where((matrix_entries >= 0)[:, None], summand_terms, jnp.zeros_like(summand_terms))
        running_totals = running_totals.at[jnp.maximum(matrix_entries, 0)].add(summand_terms)
    return running_totals


def upward(child_boxes, translation_operators):
    parents = child_boxes.shape[0] // 8
    columns = translation_operators.shape[2]
    stacked = child_boxes.reshape(parents, 8 * columns)
    merged = jnp.dot(stacked, translation_operators.reshape(8 * columns, columns), preferred_element_type=jnp.float32)
    return merged.astype(jnp.bfloat16)


def downward(parents, translation_operators):
    count_parents = parents.shape[0]
    columns = translation_operators.shape[0]
    spread = jnp.dot(parents, translation_operators.reshape(columns, 8 * columns), preferred_element_type=jnp.float32)
    return spread.astype(jnp.bfloat16).reshape(8 * count_parents, columns)


def adjoint_ascent(child_boxes, translation_operators):
    parents = child_boxes.shape[0] // 8
    columns = translation_operators.shape[0]
    stacked = child_boxes.reshape(parents, 8 * columns)
    merged = jnp.dot(stacked, translation_operators.reshape(columns, 8 * columns).T, preferred_element_type=jnp.float32)
    return merged.astype(jnp.bfloat16)


def adjoint_down(parents, translation_operators):
    count_parents = parents.shape[0]
    columns = translation_operators.shape[2]
    spread = jnp.dot(parents, translation_operators.reshape(8 * columns, columns).T, preferred_element_type=jnp.float32)
    return spread.astype(jnp.bfloat16).reshape(8 * count_parents, columns)


def reference(densities, cotangents, far_list, near_list, coarse_list, to_moments, merge_moments, far_translate, local_split, to_values, near_blocks):
    far_entries = absolute_entries(far_list)
    near_entries = absolute_entries(near_list)
    leaf_moments = jnp.dot(densities, to_moments, preferred_element_type=jnp.float32).astype(jnp.bfloat16)
    climbing = leaf_moments
    for segment_index in range(4):
        climbing = upward(climbing, merge_moments)
    coarse_local = listed_sum(climbing, coarse_list, far_translate).astype(jnp.bfloat16)
    falling = coarse_local
    for segment_index in range(4):
        falling = downward(falling, local_split)
    leaf_far = listed_sum(leaf_moments, far_entries, far_translate)
    leaf_local = (leaf_far + falling.astype(jnp.float32)).astype(jnp.bfloat16)
    near_values = listed_sum(densities, near_entries, near_blocks)
    potential = jnp.dot(leaf_local, to_values, preferred_element_type=jnp.float32) + near_values

    adjoint_local = jnp.dot(cotangents, to_values.T, preferred_element_type=jnp.float32).astype(jnp.bfloat16)
    climbing = adjoint_local
    for segment_index in range(4):
        climbing = adjoint_ascent(climbing, local_split)
    coarse_adjoint = listed_scatter(climbing, coarse_list, far_translate, climbing.shape[0]).astype(jnp.bfloat16)
    falling = coarse_adjoint
    for segment_index in range(4):
        falling = adjoint_down(falling, merge_moments)
    adjoint_far = listed_scatter(adjoint_local, far_entries, far_translate, adjoint_local.shape[0])
    adjoint_moments = (adjoint_far + falling.astype(jnp.float32)).astype(jnp.bfloat16)
    near_adjoint = listed_scatter(cotangents, near_entries, near_blocks, cotangents.shape[0])
    gradient = jnp.dot(adjoint_moments, to_moments.T, preferred_element_type=jnp.float32) + near_adjoint
    return potential, gradient
```

```python
import functools

import jax
import jax.numpy as jnp
from jax import lax
from jax.experimental import pallas as pl
from jax.experimental.pallas import tpu as pltpu
from jax.sharding import PartitionSpec as P

HW = 128
TILE = 256
AXES = ("coarse", "leaf")
F32 = jnp.float32
BF16 = jnp.bfloat16
NN = (((1,), (0,)), ((), ()))
NT = (((1,), (1,)), ((), ()))


def dot(a, b, dims=NN):
    return lax.dot_general(a, b, dims, preferred_element_type=F32)


def rounded(x):
    return x.astype(BF16).astype(F32)


def whole(count):
    return [pl.BlockSpec(memory_space=pltpu.VMEM)] * count


def get_rows(ref, at):
    return jnp.concatenate([ref[h, at, :] for h in range(ref.shape[0])], axis=1)


def put_rows(ref, at, x):
    for h in range(ref.shape[0]):
        ref[h, at, :] = x[:, h * 128 : (h + 1) * 128]


def climb_kernel(dens, cot, to_m, to_v, merge, split, out, mom, adj):
    rows = dens.shape[0]
    k = to_m.shape[1]
    put_rows(mom, pl.ds(0, rows), rounded(dot(dens[...], to_m[...])))
    put_rows(adj, pl.ds(0, rows), rounded(dot(cot[...], to_v[...], NT)))
    while rows > 1:
        rows //= 8
        up = jnp.zeros((rows, k), F32)
        adj_up = jnp.zeros((rows, k), F32)
        for c in range(8):
            child = pl.ds(c, rows, stride=8) if rows > 1 else pl.ds(c, 1)
            up += dot(get_rows(mom, child).astype(BF16), merge[c])
            adj_up += dot(get_rows(adj, child).astype(BF16), split[:, c * k : (c + 1) * k], NT)
        put_rows(mom, pl.ds(0, rows), rounded(up))
        put_rows(adj, pl.ds(0, rows), rounded(adj_up))
    row = jnp.concatenate([mom[0, :1], mom[1, :1], adj[0, :1], adj[1, :1], jnp.zeros((4, 128), F32)], axis=0)
    out[...] = jnp.broadcast_to(row[None], (out.shape[0] // 8, 8, 128)).reshape(out.shape)


def near_far_kernel(
    place, far, near, dens, cot, recv_e, recv_o, to_m, to_v, far_w, near_w,
    leaf_far, near_val, adj_far, near_adj,
    dens_wide, cot_wide, mom_wide, adj_wide, row_targets, col_targets,
):
    rows = dens.shape[0]
    wide = rows + 2 * HW
    n_far, n_near = far.shape[0], near.shape[0]
    slots = n_far + n_near
    odd = lax.rem(place[0], 2) == 1
    first, second = recv_e[...], recv_o[...]
    left = jnp.where(odd, first, second)
    right = jnp.where(odd, second, first)
    for target, own, start in ((dens_wide, dens, 0), (cot_wide, cot, HW)):
        target[:HW, :] = left[start : start + HW]
        target[HW : HW + rows, :] = own[...]
        target[HW + rows :, :] = right[start : start + HW]
    mom_wide[...] = dot(dens_wide[...], to_m[...]).astype(BF16)
    adj_wide[...] = dot(cot_wide[...], to_v[...], NT).astype(BF16)

    padded = row_targets.shape[0]
    row_targets[...] = jnp.full(row_targets.shape, -1.0, F32)
    row_targets[:, :HW] = left[2 * HW :].astype(F32)
    row_targets[:n_far, HW : HW + rows] = far[...].astype(F32)
    row_targets[n_far:slots, HW : HW + rows] = near[...].astype(F32)
    row_targets[:, HW + rows :] = right[2 * HW :].astype(F32)
    own = row_targets[:, HW : HW + rows]
    own = jnp.concatenate([own, jnp.full((128 - padded, rows), -1.0, F32)], axis=0)
    own = own.T
    place_r = (lax.broadcasted_iota(jnp.int32, own.shape, 0) % TILE).astype(F32)
    col_targets[...] = jnp.where(own >= 0, own + place_r, -1.0)
    entries = row_targets[...]
    place_w = (lax.broadcasted_iota(jnp.int32, entries.shape, 1) % TILE).astype(F32)
    row_targets[...] = jnp.where(entries >= 0, entries + place_w, -1.0)

    leaf_far[...] = jnp.zeros(leaf_far.shape, F32)
    near_val[...] = jnp.zeros(near_val.shape, F32)
    adj_far[...] = jnp.zeros(adj_far.shape, F32)
    near_adj[...] = jnp.zeros(near_adj.shape, F32)
    lane = lax.broadcasted_iota(jnp.int32, (TILE, 128), 1).astype(F32)
    lanes = [lane.astype(BF16), (lane + 128.0).astype(BF16)]
    down = lax.broadcasted_iota(jnp.int32, (TILE, TILE), 0).astype(F32).astype(BF16)
    one = jnp.ones((), BF16)
    zero = jnp.zeros((), BF16)

    def step(slot, operator, fwd_src, fwd_out, adj_src, adj_out):
        for p in range(rows // TILE):
            own = pl.ds(p * TILE, TILE)
            reach = pl.ds(p * TILE, 2 * TILE)
            column = col_targets[own, :]
            column = jnp.take_along_axis(column, jnp.full(column.shape, slot, jnp.int32), axis=1)
            low, high = column.astype(BF16), (column - TILE).astype(BF16)
            table = jnp.concatenate(
                [jnp.where(c == t, one, zero) for t in (low, high) for c in lanes], axis=1
            )
            picked = dot(table, fwd_src[reach, :]).astype(BF16)
            fwd_out[own, :] += dot(picked, operator)
            entry = row_targets[pl.ds(slot, 1), p * TILE : (p + 2) * TILE]
            high = jnp.broadcast_to(entry[:, :TILE] - TILE, (TILE, TILE)).astype(BF16)
            low = jnp.broadcast_to(entry[:, TILE:], (TILE, TILE)).astype(BF16)
            table = jnp.concatenate(
                [jnp.where(down == t, one, zero) for t in (high, low)], axis=1
            )
            collected = dot(table, adj_src[reach, :]).astype(BF16)
            adj_out[own, :] += dot(collected, operator, NT)

    @pl.loop(0, n_far)
    def _(j):
        step(j, far_w[j], mom_wide, leaf_far, adj_wide, adj_far)

    @pl.loop(0, n_near)
    def _(j):
        step(j + n_far, near_w[j], dens_wide, near_val, cot_wide, near_adj)


def fall_kernel(
    place, gathered, coarse_list, coarse_list_t, merge, far_w, split, to_m, to_v,
    leaf_far, near_val, adj_far, near_adj,
    potential, gradient,
    fall, adj_fall,
):
    k = merge.shape[2]
    boxes = coarse_list.shape[1]
    coarse_m = jnp.zeros((boxes, k), F32)
    coarse_a = jnp.zeros((boxes, k), F32)
    for c in range(8):
        parts = [gathered[pl.ds(8 * c + i, boxes, stride=64), :] for i in range(4)]
        moments = jnp.concatenate(parts[:2], axis=1).astype(BF16)
        adjoints = jnp.concatenate(parts[2:], axis=1).astype(BF16)
        coarse_m += dot(moments, merge[c])
        coarse_a += dot(adjoints, split[:, c * k : (c + 1) * k], NT)
    coarse_m = coarse_m.astype(BF16)
    coarse_a = coarse_a.astype(BF16)
    local = jnp.zeros((boxes, k), F32)
    adjoint = jnp.zeros((boxes, k), F32)
    across = lax.broadcasted_iota(jnp.int32, (boxes, boxes), 1)
    along = lax.broadcasted_iota(jnp.int32, (boxes, boxes), 0)
    for j in range(far_w.shape[0]):
        table = jnp.where(across == coarse_list_t[:, j : j + 1], 1.0, 0.0).astype(BF16)
        local += dot(dot(table, coarse_m).astype(BF16), far_w[j])
        table = jnp.where(along == coarse_list[j : j + 1, :], 1.0, 0.0).astype(BF16)
        adjoint += dot(dot(table, coarse_a).astype(BF16), far_w[j], NT)
    put_rows(fall, pl.ds(0, boxes), rounded(local))
    put_rows(adj_fall, pl.ds(0, boxes), rounded(adjoint))
    box, child = place[0] // 8, lax.rem(place[0], 8)
    top = get_rows(fall, pl.ds(box, 1)).astype(BF16)
    adj_top = get_rows(adj_fall, pl.ds(box, 1)).astype(BF16)
    put_rows(fall, pl.ds(0, 1), rounded(dot(top, split[:, pl.ds(pl.multiple_of(child * k, k), k)])))
    put_rows(adj_fall, pl.ds(0, 1), rounded(dot(adj_top, merge[child], NT)))
    rows = 1
    while rows < fall.shape[1]:
        parents = get_rows(fall, pl.ds(0, rows)).astype(BF16)
        adj_parents = get_rows(adj_fall, pl.ds(0, rows)).astype(BF16)
        for c in range(8):
            children = pl.ds(c, rows, stride=8) if rows > 1 else pl.ds(c, 1)
            put_rows(fall, children, rounded(dot(parents, split[:, c * k : (c + 1) * k])))
            put_rows(adj_fall, children, rounded(dot(adj_parents, merge[c], NT)))
        rows *= 8
    potential[...] = dot((leaf_far[...] + get_rows(fall, pl.ds(0, rows))).astype(BF16), to_v[...]) + near_val[...]
    gradient[...] = dot((adj_far[...] + get_rows(adj_fall, pl.ds(0, rows))).astype(BF16), to_m[...], NT) + near_adj[...]


def edge(odd, densities, cotangents, lists):
    rows = densities.shape[0]
    at = jnp.where(odd, rows - HW, 0)
    return jnp.concatenate(
        [
            lax.dynamic_slice_in_dim(densities, at, HW, 0),
            lax.dynamic_slice_in_dim(cotangents, at, HW, 0),
            lax.dynamic_slice_in_dim(lists, at, HW, 1),
        ],
        axis=0,
    )


def per_device(
    densities, cotangents, far_list, near_list, coarse_list,
    to_moments, merge_moments, far_translate, local_split, to_values, near_blocks,
):
    rows = densities.shape[0]
    k = to_moments.shape[1]
    count = lax.axis_size(AXES)
    here = lax.axis_index(AXES)
    place = here.astype(jnp.int32).reshape(1)
    odd = lax.rem(here, 2) == 1
    slots = far_list.shape[0] + near_list.shape[0]
    padded = -(-slots // 16) * 16
    lists = jnp.concatenate(
        [far_list, near_list, jnp.full((padded - slots, rows), -1, jnp.int32)], axis=0
    ).astype(BF16)
    recv_e = lax.ppermute(
        edge(~odd, densities, cotangents, lists), AXES, [(i, i ^ 1) for i in range(count)]
    )
    pairs = [(i, i + 1) for i in range(1, count - 1, 2)]
    recv_o = lax.ppermute(
        edge(odd, densities, cotangents, lists), AXES, pairs + [(b, a) for a, b in pairs]
    )
    split = local_split.reshape(k, 8 * k)
    smem = pl.BlockSpec(memory_space=pltpu.SMEM)

    row = pl.pallas_call(
        climb_kernel,
        out_shape=jax.ShapeDtypeStruct((count * 8, 128), F32),
        in_specs=whole(6),
        out_specs=pl.BlockSpec(memory_space=pltpu.VMEM),
        scratch_shapes=[pltpu.VMEM((k // 128, rows, 128), F32)] * 2,
        compiler_params=pltpu.CompilerParams(vmem_limit_bytes=16 << 20),
        name="climb",
    )(densities, cotangents, to_moments, to_values, merge_moments, split)
    gathered = lax.all_to_all(row, AXES, 0, 0, tiled=True)

    wide = rows + 2 * HW
    sums = pl.pallas_call(
        near_far_kernel,
        out_shape=[
            jax.ShapeDtypeStruct((rows, k), F32),
            jax.ShapeDtypeStruct((rows, 128), F32),
            jax.ShapeDtypeStruct((rows, k), F32),
            jax.ShapeDtypeStruct((rows, 128), F32),
        ],
        in_specs=[smem] + whole(10),
        out_specs=whole(4),
        scratch_shapes=[
            pltpu.VMEM((wide, 128), BF16),
            pltpu.VMEM((wide, 128), BF16),
            pltpu.VMEM((wide, k), BF16),
            pltpu.VMEM((wide, k), BF16),
            pltpu.VMEM((padded, wide), F32),
            pltpu.VMEM((rows, 128), F32),
        ],
        compiler_params=pltpu.CompilerParams(vmem_limit_bytes=40 << 20),
        cost_estimate=pl.CostEstimate(flops=20 * 10**9, bytes_accessed=5 << 20, transcendentals=0),
        name="near_far",
    )(
        place, far_list, near_list, densities, cotangents, recv_e, recv_o,
        to_moments, to_values, far_translate, near_blocks,
    )

    return pl.pallas_call(
        fall_kernel,
        out_shape=[jax.ShapeDtypeStruct((rows, 128), F32)] * 2,
        in_specs=[smem] + whole(12),
        out_specs=whole(2),
        scratch_shapes=[pltpu.VMEM((k // 128, rows, 128), F32)] * 2,
        compiler_params=pltpu.CompilerParams(vmem_limit_bytes=24 << 20),
        name="fall",
    )(
        place, gathered, coarse_list, coarse_list.T, merge_moments, far_translate, split,
        to_moments, to_values, *sums,
    )


def solution(mesh):
    rows = P(AXES, None)
    lists = P(None, AXES)
    return jax.shard_map(
        per_device,
        mesh=mesh,
        in_specs=(rows, rows, lists, lists) + (P(),) * 7,
        out_specs=(rows, rows),
        check_vma=False,
    )
```

```python
import functools

import jax
import jax.numpy as jnp
from jax import lax
from jax.experimental import pallas as pl
from jax.experimental.pallas import tpu as pltpu
from jax.sharding import PartitionSpec as P

HW = 128
TILE = 256
AXES = ("coarse", "leaf")
F32 = jnp.float32
BF16 = jnp.bfloat16
NN = (((1,), (0,)), ((), ()))
NT = (((1,), (1,)), ((), ()))


def dot(a, b, dims=NN):
    return lax.dot_general(a, b, dims, preferred_element_type=F32)


def rounded(x):
    return x.astype(BF16).astype(F32)


def anywhere(count):
    return [pl.BlockSpec(memory_space=pl.ANY)] * count


def in_vmem(count):
    return [pl.BlockSpec(memory_space=pltpu.VMEM)] * count


def held(*arrays):
    return [pltpu.VMEM(a.shape, a.dtype) for a in arrays] + [pltpu.SemaphoreType.DMA((len(arrays),))]


class Fetch:
    def __init__(self, sources, targets, sems):
        self.copies = [
            pltpu.make_async_copy(s, t, sems.at[i]) for i, (s, t) in enumerate(zip(sources, targets))
        ]
        for copy in self.copies:
            copy.start()

    def wait(self, *which):
        for i in which:
            self.copies[i].wait()


def get_rows(ref, at):
    return jnp.concatenate([ref[h, at, :] for h in range(ref.shape[0])], axis=1)


def put_rows(ref, at, x):
    for h in range(ref.shape[0]):
        ref[h, at, :] = x[:, h * 128 : (h + 1) * 128]


def here():
    return lax.axis_index(AXES)


def rim(last, dens, cot, far, near, out):
    rows = dens.shape[0]
    pad = out.shape[0] - 2 * HW - far.shape[0] - near.shape[0]
    ends = []
    for at in (slice(rows - HW, rows), slice(0, HW)):
        lists = [far[:, at].astype(F32), near[:, at].astype(F32), jnp.full((pad, HW), -1.0, F32)]
        ends.append(jnp.concatenate(lists, axis=0).astype(BF16))
    out[:HW, :] = jnp.where(last, dens[rows - HW :, :], dens[:HW, :])
    out[HW : 2 * HW, :] = jnp.where(last, cot[rows - HW :, :], cot[:HW, :])
    out[2 * HW :, :] = jnp.where(last, ends[0], ends[1])


def climb_kernel(*refs):
    sources, (out, far_rim, near_rim, split_by_child), rest = refs[:8], refs[8:12], refs[12:]
    dens, cot, far, near, to_m, to_v, merge, split, sems, mom, adj, wide = rest
    fetch = Fetch(sources, rest[:8], sems)
    rows = dens.shape[0]
    k = to_m.shape[1]
    odd = lax.rem(here(), 2) == 1
    fetch.wait(0, 1, 2, 3)
    rim(odd, dens, cot, far, near, far_rim)
    rim(jnp.logical_not(odd), dens, cot, far, near, near_rim)
    fetch.wait(4, 5)
    put_rows(mom, pl.ds(0, rows), rounded(dot(dens[...], to_m[...])))
    put_rows(adj, pl.ds(0, rows), rounded(dot(cot[...], to_v[...], NT)))
    fetch.wait(6, 7)
    for h in range(2):
        wide[h] = split[:, :, h * 128 : (h + 1) * 128].astype(F32).reshape(8 * k, 128)
    for c in range(8):
        split_by_child[c] = get_rows(wide, pl.ds(c, k, stride=8)).astype(BF16)
    while rows > 1:
        rows //= 8
        up = jnp.zeros((rows, k), F32)
        adj_up = jnp.zeros((rows, k), F32)
        for c in range(8):
            child = pl.ds(c, rows, stride=8) if rows > 1 else pl.ds(c, 1)
            up += dot(get_rows(mom, child).astype(BF16), merge[c])
            adj_up += dot(get_rows(adj, child).astype(BF16), split_by_child[c], NT)
        put_rows(mom, pl.ds(0, rows), rounded(up))
        put_rows(adj, pl.ds(0, rows), rounded(adj_up))
    row = jnp.concatenate([mom[0, :1], mom[1, :1], adj[0, :1], adj[1, :1], jnp.zeros((4, 128), F32)], axis=0)
    out[...] = jnp.broadcast_to(row[None], (out.shape[0] // 8, 8, 128)).reshape(out.shape)


def near_far_kernel(*refs):
    sources, (potential, gradient), rest = refs[:10], refs[10:12], refs[12:]
    recv_e, recv_o, far, near, dens, cot, to_m, to_v, far_w, near_w, sems = rest[:11]
    dens_wide, cot_wide, mom_wide, adj_wide, row_targets, col_targets = rest[11:17]
    dens_pair, far_picked, far_collected, near_picked, near_collected, far_wt, near_wt = rest[17:]
    fetch = Fetch(sources, rest[:10], sems)
    fetch.wait(0, 1, 2, 3, 4, 5, 6, 7)
    rows = dens.shape[0]
    wide = rows + 2 * HW
    n_far, n_near = far.shape[0], near.shape[0]
    slots = n_far + n_near
    odd = lax.rem(here(), 2) == 1
    first, second = recv_e[...], recv_o[...]
    left = jnp.where(odd, first, second)
    right = jnp.where(odd, second, first)
    for target, own, start in ((dens_wide, dens, 0), (cot_wide, cot, HW)):
        target[:HW, :] = left[start : start + HW]
        target[HW : HW + rows, :] = own[...]
        target[HW + rows :, :] = right[start : start + HW]
    mom_wide[...] = dot(dens_wide[...], to_m[...]).astype(BF16)
    adj_wide[...] = dot(cot_wide[...], to_v[...], NT).astype(BF16)

    padded = row_targets.shape[0]
    row_targets[...] = jnp.full(row_targets.shape, -1.0, F32)
    row_targets[:, :HW] = left[2 * HW :].astype(F32)
    row_targets[:n_far, HW : HW + rows] = far[...].astype(F32)
    row_targets[n_far:slots, HW : HW + rows] = near[...].astype(F32)
    row_targets[:, HW + rows :] = right[2 * HW :].astype(F32)
    own = row_targets[:, HW : HW + rows]
    own = jnp.concatenate([own, jnp.full((128 - padded, rows), -1.0, F32)], axis=0)
    own = own.T
    place_r = (lax.broadcasted_iota(jnp.int32, own.shape, 0) % TILE).astype(F32)
    col_targets[...] = jnp.where(own >= 0, own + place_r, -1.0)
    entries = row_targets[...]
    place_w = (lax.broadcasted_iota(jnp.int32, entries.shape, 1) % TILE).astype(F32)
    row_targets[...] = jnp.where(entries >= 0, entries + place_w, -1.0)

    lane = lax.broadcasted_iota(jnp.int32, (TILE, 128), 1).astype(F32)
    lanes = [lane.astype(BF16), (lane + 128.0).astype(BF16)]
    down = lax.broadcasted_iota(jnp.int32, (TILE, TILE), 0).astype(F32).astype(BF16)
    one = jnp.ones((), BF16)
    zero = jnp.zeros((), BF16)
    blocks = rows // TILE
    for p in range(blocks):
        dens_pair[p, :, :128] = dens_wide[p * TILE : (p + 1) * TILE, :]
        dens_pair[p, :, 128:] = dens_wide[(p + 1) * TILE : (p + 2) * TILE, :]

    def column_of(slot, p):
        column = col_targets[p * TILE : (p + 1) * TILE, :]
        return jnp.take_along_axis(column, jnp.full(column.shape, slot, jnp.int32), axis=1)

    def table_of(slot, p):
        column = column_of(slot, p)
        low, high = column.astype(BF16), (column - TILE).astype(BF16)
        return jnp.concatenate(
            [jnp.where(c == t, one, zero) for t in (low, high) for c in lanes], axis=1
        )

    def scatter_table_of(slot, p):
        entry = row_targets[pl.ds(slot, 1), p * TILE : (p + 2) * TILE]
        high = jnp.broadcast_to(entry[:, :TILE] - TILE, (TILE, TILE)).astype(BF16)
        low = jnp.broadcast_to(entry[:, TILE:], (TILE, TILE)).astype(BF16)
        return jnp.concatenate([jnp.where(down == t, one, zero) for t in (high, low)], axis=1)

    fetch.wait(8, 9)

    @pl.loop(0, n_far, unroll=4)
    def _(j):
        at = pl.ds(pl.multiple_of(j * TILE, TILE), TILE)
        for p in range(blocks):
            own, reach = pl.ds(p * TILE, TILE), pl.ds(p * TILE, 2 * TILE)
            far_picked[own, at] = dot(table_of(j, p), mom_wide[reach, :]).astype(BF16)
            far_collected[own, at] = dot(scatter_table_of(j, p), adj_wide[reach, :]).astype(BF16)
        far_wt[pl.ds(pl.multiple_of(j * TILE, TILE), TILE), :] = far_w[j].T

    @pl.loop(0, n_near, unroll=9)
    def _(j):
        at = pl.ds(pl.multiple_of(j * 128, 128), 128)
        for p in range(blocks):
            own, reach = pl.ds(p * TILE, TILE), pl.ds(p * TILE, 2 * TILE)
            column = column_of(j + n_far, p)
            second = column >= TILE
            place = jnp.where(second, column - TILE, column).astype(BF16)
            table = jnp.concatenate([jnp.where(c == place, one, zero) for c in lanes], axis=1)
            both = dot(table, dens_pair[p])
            near_picked[own, at] = jnp.where(second, both[:, 128:], both[:, :128]).astype(BF16)
            near_collected[own, at] = dot(scatter_table_of(j + n_far, p), cot_wide[reach, :]).astype(BF16)
        near_wt[pl.ds(pl.multiple_of(j * 128, 128), 128), :] = near_w[j].T

    leaf_far = dot(far_picked[...], far_w[...].reshape(far_wt.shape)).astype(BF16)
    adj_far = dot(far_collected[...], far_wt[...]).astype(BF16)
    near_val = dot(near_picked[...], near_w[...].reshape(near_wt.shape))
    near_adj = dot(near_collected[...], near_wt[...])
    potential[...] = dot(leaf_far, to_v[...]) + near_val
    gradient[...] = dot(adj_far, to_m[...], NT) + near_adj


def fall_kernel(*refs):
    sources, (potential, gradient), rest = refs[:9], refs[9:11], refs[11:]
    gathered, coarse_list, merge, split, far_w, to_m, to_v, near_pot, near_grad, sems, fall, adj_fall = rest
    fetch = Fetch(sources, rest[:9], sems)
    fetch.wait(0, 1, 2, 3)
    k = merge.shape[2]
    boxes = coarse_list.shape[1]
    coarse_m = jnp.zeros((boxes, k), F32)
    coarse_a = jnp.zeros((boxes, k), F32)
    for c in range(8):
        parts = [gathered[pl.ds(8 * c + i, boxes, stride=64), :] for i in range(4)]
        moments = jnp.concatenate(parts[:2], axis=1).astype(BF16)
        adjoints = jnp.concatenate(parts[2:], axis=1).astype(BF16)
        coarse_m += dot(moments, merge[c])
        coarse_a += dot(adjoints, split[c], NT)
    coarse_m = coarse_m.astype(BF16)
    coarse_a = coarse_a.astype(BF16)
    local = jnp.zeros((boxes, k), F32)
    adjoint = jnp.zeros((boxes, k), F32)
    fetch.wait(4)
    coarse_list_t = jnp.concatenate(
        [coarse_list[...].astype(F32), jnp.full((boxes, 128 - boxes), -1.0, F32)], axis=1
    )
    coarse_list_t = jnp.concatenate([coarse_list_t, jnp.full((128 - boxes, 128), -1.0, F32)], axis=0).T
    coarse_list_t = coarse_list_t[:boxes, :].astype(jnp.int32)
    across = lax.broadcasted_iota(jnp.int32, (boxes, boxes), 1)
    along = lax.broadcasted_iota(jnp.int32, (boxes, boxes), 0)
    for j in range(far_w.shape[0]):
        table = jnp.where(across == coarse_list_t[:, j : j + 1], 1.0, 0.0).astype(BF16)
        local += dot(dot(table, coarse_m).astype(BF16), far_w[j])
        table = jnp.where(along == coarse_list[j : j + 1, :], 1.0, 0.0).astype(BF16)
        adjoint += dot(dot(table, coarse_a).astype(BF16), far_w[j], NT)
    put_rows(fall, pl.ds(0, boxes), rounded(local))
    put_rows(adj_fall, pl.ds(0, boxes), rounded(adjoint))
    box, child = here() // 8, lax.rem(here(), 8)
    top = get_rows(fall, pl.ds(box, 1)).astype(BF16)
    adj_top = get_rows(adj_fall, pl.ds(box, 1)).astype(BF16)
    put_rows(fall, pl.ds(0, 1), rounded(dot(top, split[child])))
    put_rows(adj_fall, pl.ds(0, 1), rounded(dot(adj_top, merge[child], NT)))
    rows = 1
    while rows < fall.shape[1]:
        parents = get_rows(fall, pl.ds(0, rows)).astype(BF16)
        adj_parents = get_rows(adj_fall, pl.ds(0, rows)).astype(BF16)
        for c in range(8):
            children = pl.ds(c, rows, stride=8) if rows > 1 else pl.ds(c, 1)
            put_rows(fall, children, rounded(dot(parents, split[c])))
            put_rows(adj_fall, children, rounded(dot(adj_parents, merge[c], NT)))
        rows *= 8
    fetch.wait(5, 6, 7, 8)
    potential[...] = dot(get_rows(fall, pl.ds(0, rows)).astype(BF16), to_v[...]) + near_pot[...]
    gradient[...] = dot(get_rows(adj_fall, pl.ds(0, rows)).astype(BF16), to_m[...], NT) + near_grad[...]


def near_far_call(far, near, dens, cot, recv_e, recv_o, to_m, to_v, far_w, near_w):
    rows = dens.shape[0]
    k = to_m.shape[1]
    padded = recv_e.shape[0] - 2 * HW
    wide = rows + 2 * HW
    operands = (recv_e, recv_o, far, near, dens, cot, to_m, to_v, far_w, near_w)
    return pl.pallas_call(
        near_far_kernel,
        out_shape=[jax.ShapeDtypeStruct((rows, 128), F32)] * 2,
        in_specs=anywhere(10),
        out_specs=in_vmem(2),
        scratch_shapes=held(*operands)
        + [
            pltpu.VMEM((wide, 128), BF16),
            pltpu.VMEM((wide, 128), BF16),
            pltpu.VMEM((wide, k), BF16),
            pltpu.VMEM((wide, k), BF16),
            pltpu.VMEM((padded, wide), F32),
            pltpu.VMEM((rows, 128), F32),
            pltpu.VMEM((rows // TILE, TILE, 256), BF16),
            pltpu.VMEM((rows, far.shape[0] * k), BF16),
            pltpu.VMEM((rows, far.shape[0] * k), BF16),
            pltpu.VMEM((rows, near.shape[0] * 128), BF16),
            pltpu.VMEM((rows, near.shape[0] * 128), BF16),
            pltpu.VMEM((far.shape[0] * k, k), BF16),
            pltpu.VMEM((near.shape[0] * 128, 128), BF16),
        ],
        compiler_params=pltpu.CompilerParams(vmem_limit_bytes=64 << 20),
        cost_estimate=pl.CostEstimate(flops=20 * 10**9, bytes_accessed=5 << 20, transcendentals=0),
        name="near_far",
    )(*operands)


def per_device(
    densities, cotangents, far_list, near_list, coarse_list,
    to_moments, merge_moments, far_translate, local_split, to_values, near_blocks,
):
    rows = densities.shape[0]
    k = to_moments.shape[1]
    count = lax.axis_size(AXES)
    slots = far_list.shape[0] + near_list.shape[0]
    rim_shape = jax.ShapeDtypeStruct((2 * HW + -(-slots // 16) * 16, 128), BF16)
    chain = pltpu.VMEM((k // 128, rows, 128), F32)
    operands = (
        densities, cotangents, far_list, near_list, to_moments, to_values, merge_moments, local_split,
    )
    row, far_rim, near_rim, split = pl.pallas_call(
        climb_kernel,
        out_shape=[
            jax.ShapeDtypeStruct((count * 8, 128), F32),
            rim_shape,
            rim_shape,
            jax.ShapeDtypeStruct((8, k, k), BF16),
        ],
        in_specs=anywhere(8),
        out_specs=in_vmem(4),
        scratch_shapes=held(*operands) + [chain, chain, pltpu.VMEM((k // 128, 8 * k, 128), F32)],
        compiler_params=pltpu.CompilerParams(vmem_limit_bytes=64 << 20),
        name="climb",
    )(*operands)
    pairs = [(i, i + 1) for i in range(1, count - 1, 2)]
    recv_o = lax.ppermute(far_rim, AXES, pairs + [(b, a) for a, b in pairs])
    recv_e = lax.ppermute(near_rim, AXES, [(i, i ^ 1) for i in range(count)])
    gathered = lax.all_to_all(row, AXES, 0, 0, tiled=True)
    sums = near_far_call(
        far_list, near_list, densities, cotangents, recv_e, recv_o,
        to_moments, to_values, far_translate, near_blocks,
    )
    operands = (
        gathered, coarse_list, merge_moments, split, far_translate, to_moments, to_values, *sums,
    )
    return pl.pallas_call(
        fall_kernel,
        out_shape=[jax.ShapeDtypeStruct((rows, 128), F32)] * 2,
        in_specs=anywhere(9),
        out_specs=in_vmem(2),
        scratch_shapes=held(*operands) + [chain, chain],
        compiler_params=pltpu.CompilerParams(vmem_limit_bytes=64 << 20),
        name="fall",
    )(*operands)


def solution(mesh):
    rows = P(AXES, None)
    lists = P(None, AXES)
    return jax.shard_map(
        per_device,
        mesh=mesh,
        in_specs=(rows, rows, lists, lists) + (P(),) * 7,
        out_specs=(rows, rows),
        check_vma=False,
    )
```

```python
import functools

import jax
import jax.numpy as jnp
from jax import lax
from jax.experimental import pallas as pl
from jax.experimental.pallas import tpu as pltpu
from jax.sharding import PartitionSpec as P

HW = 128
TILE = 256
PAIR = 8
AXES = ("coarse", "leaf")
F32 = jnp.float32
BF16 = jnp.bfloat16
NN = (((1,), (0,)), ((), ()))
NT = (((1,), (1,)), ((), ()))


def dot(a, b, dims=NN):
    return lax.dot_general(a, b, dims, preferred_element_type=F32)


def rounded(x):
    return x.astype(BF16).astype(F32)


def anywhere(count):
    return [pl.BlockSpec(memory_space=pl.ANY)] * count


def in_vmem(count):
    return [pl.BlockSpec(memory_space=pltpu.VMEM)] * count


def held(*arrays):
    return [pltpu.VMEM(a.shape, a.dtype) for a in arrays] + [pltpu.SemaphoreType.DMA((len(arrays),))]


class Fetch:
    def __init__(self, sources, targets, sems):
        self.copies = [
            pltpu.make_async_copy(s, t, sems.at[i]) for i, (s, t) in enumerate(zip(sources, targets))
        ]
        for copy in self.copies:
            copy.start()

    def wait(self, *which):
        for i in which:
            self.copies[i].wait()


def get_rows(ref, at):
    return jnp.concatenate([ref[h, at, :] for h in range(ref.shape[0])], axis=1)


def put_rows(ref, at, x):
    for h in range(ref.shape[0]):
        ref[h, at, :] = x[:, h * 128 : (h + 1) * 128]


def here():
    return lax.axis_index(AXES)


def rim(last, dens, cot, far, near, out):
    rows = dens.shape[0]
    pad = out.shape[0] - 2 * HW - far.shape[0] - near.shape[0]
    ends = []
    for at in (slice(rows - HW, rows), slice(0, HW)):
        lists = [far[:, at].astype(F32), near[:, at].astype(F32), jnp.full((pad, HW), -1.0, F32)]
        ends.append(jnp.concatenate(lists, axis=0).astype(BF16))
    out[:HW, :] = jnp.where(last, dens[rows - HW :, :], dens[:HW, :])
    out[HW : 2 * HW, :] = jnp.where(last, cot[rows - HW :, :], cot[:HW, :])
    out[2 * HW :, :] = jnp.where(last, ends[0], ends[1])


def climb_kernel(*refs):
    sources, (out, far_rim, near_rim, split_by_child), rest = refs[:8], refs[8:12], refs[12:]
    dens, cot, far, near, to_m, to_v, merge, split, sems, mom, adj, wide = rest
    fetch = Fetch(sources, rest[:8], sems)
    rows = dens.shape[0]
    k = to_m.shape[1]
    odd = lax.rem(here(), 2) == 1
    fetch.wait(0, 1, 2, 3)
    rim(odd, dens, cot, far, near, far_rim)
    rim(jnp.logical_not(odd), dens, cot, far, near, near_rim)
    fetch.wait(4, 5)
    put_rows(mom, pl.ds(0, rows), rounded(dot(dens[...], to_m[...])))
    put_rows(adj, pl.ds(0, rows), rounded(dot(cot[...], to_v[...], NT)))
    fetch.wait(6, 7)
    for h in range(2):
        wide[h] = split[:, :, h * 128 : (h + 1) * 128].astype(F32).reshape(8 * k, 128)
    for c in range(8):
        split_by_child[c] = get_rows(wide, pl.ds(c, k, stride=8)).astype(BF16)
    while rows > 1:
        rows //= 8
        adj_up = jnp.zeros((rows, k), F32)
        children = [pl.ds(c, rows, stride=8) if rows > 1 else pl.ds(c, 1) for c in range(8)]
        up = jnp.concatenate([get_rows(mom, child) for child in children], axis=1).astype(BF16)
        up = dot(up, merge[...].reshape(8 * k, k))
        for c, child in enumerate(children):
            adj_up += dot(get_rows(adj, child).astype(BF16), split_by_child[c], NT)
        put_rows(mom, pl.ds(0, rows), rounded(up))
        put_rows(adj, pl.ds(0, rows), rounded(adj_up))
    row = jnp.concatenate([mom[0, :1], mom[1, :1], adj[0, :1], adj[1, :1], jnp.zeros((4, 128), F32)], axis=0)
    out[...] = jnp.broadcast_to(row[None], (out.shape[0] // 8, 8, 128)).reshape(out.shape)


def near_far_kernel(*refs):
    sources, (potential, gradient), rest = refs[:10], refs[10:12], refs[12:]
    recv_e, recv_o, far, near, dens, cot, near_w, to_m, to_v, far_w, sems = rest[:11]
    dens_pair, cot_rim, row_place, rim_place, col_targets, picked, collected = rest[11:18]
    near_wt, far_half, far_op, far_opt = rest[18:]
    fetch = Fetch(sources, rest[:10], sems)
    rows = dens.shape[0]
    blocks = rows // TILE
    n_far, n_near = far.shape[0], near.shape[0]
    slots = n_far + n_near
    padded = row_place.shape[0]
    fetch.wait(0, 1, 2, 3, 4, 5)
    odd = lax.rem(here(), 2) == 1
    first, second = recv_e[...], recv_o[...]
    left = jnp.where(odd, first, second)
    right = jnp.where(odd, second, first)
    dens_wide = [left[:HW]] + [dens[i * HW : (i + 1) * HW, :] for i in range(rows // HW)] + [right[:HW]]
    for p in range(blocks):
        for i in range(4):
            at = slice((i % 2) * HW, (i % 2 + 1) * HW)
            dens_pair[p, at, (i // 2) * 128 : (i // 2 + 1) * 128] = dens_wide[2 * p + i]
    cot_rim[...] = jnp.zeros(cot_rim.shape, BF16)
    cot_rim[:HW, :128] = left[HW : 2 * HW]
    cot_rim[HW:, 128:] = right[HW : 2 * HW]

    listed = jnp.concatenate(
        [far[...].astype(F32), near[...].astype(F32), jnp.full((128 - slots, rows), -1.0, F32)], axis=0
    )
    place = (lax.broadcasted_iota(jnp.int32, listed.shape, 1) % TILE).astype(F32)
    listed = jnp.where(listed >= 0, listed + place, -1.0)
    col_targets[...] = listed.T
    listed = listed[:padded]
    row_place[...] = jnp.where(listed >= TILE, listed - TILE, listed)
    listed = jnp.concatenate([left[2 * HW :].astype(F32), right[2 * HW :].astype(F32)], axis=1)
    lane = lax.broadcasted_iota(jnp.int32, listed.shape, 1)
    place = jnp.where(lane < HW, lane - TILE, lane - HW).astype(F32)
    rim_place[...] = jnp.where(listed >= 0, listed + place, -1.0)

    lane = lax.broadcasted_iota(jnp.int32, (TILE, 128), 1).astype(F32)
    lanes = [lane.astype(BF16), (lane + 128.0).astype(BF16)]
    down = lax.broadcasted_iota(jnp.int32, (TILE, TILE), 0).astype(F32).astype(BF16)
    one = jnp.ones((), BF16)
    zero = jnp.zeros((), BF16)

    def step(slot):
        at = pl.ds(pl.multiple_of(slot * 128, 128), 128)
        parts = []
        for p in range(blocks):
            own = slice(p * TILE, (p + 1) * TILE)
            column = col_targets[own, :]
            column = jnp.take_along_axis(column, jnp.full(column.shape, slot, jnp.int32), axis=1)
            upper = column >= TILE
            place = jnp.where(upper, column - TILE, column).astype(BF16)
            table = jnp.concatenate([jnp.where(c == place, one, zero) for c in lanes], axis=1)
            both = dot(table, dens_pair[p])
            picked[own, at] = jnp.where(upper, both[:, 128:], both[:, :128]).astype(BF16)
            upper = column.astype(BF16) >= jnp.full((), TILE, BF16)
            values = cot[own, :]
            halves = [jnp.where(upper, zero, values), jnp.where(upper, values, zero)]
            entry = jnp.broadcast_to(row_place[pl.ds(slot, 1), own], (TILE, TILE)).astype(BF16)
            parts.append(dot(jnp.where(down == entry, one, zero), jnp.concatenate(halves, axis=1)))
        entry = jnp.broadcast_to(rim_place[pl.ds(slot, 1), :], (HW, TILE)).astype(BF16)
        rim = dot(jnp.where(down[:HW] == entry, one, zero), cot_rim[...])
        collected[:HW, at] = (parts[0][HW:, :128] + rim[:, :128]).astype(BF16)
        for p in range(blocks - 1):
            own = slice(HW + p * TILE, HW + (p + 1) * TILE)
            collected[own, at] = (parts[p][:, 128:] + parts[p + 1][:, :128]).astype(BF16)
        collected[rows - HW :, at] = (parts[-1][:HW, 128:] + rim[:, 128:]).astype(BF16)

    @pl.loop(0, n_far, unroll=16)
    def _(j):
        step(j)

    fetch.wait(6)

    @pl.loop(0, n_near, unroll=27)
    def _(j):
        step(j + n_far)
        near_wt[pl.ds(pl.multiple_of(j * 128, 128), 128), :] = near_w[j].T

    fetch.wait(7, 8, 9)
    for j in range(n_far):
        far_half[j * 128 : (j + 1) * 128, :] = dot(to_m[...], far_w[j]).astype(BF16)
    operator = dot(far_half[...], to_v[...])
    far_op[...] = operator.astype(BF16)
    for j in range(n_far):
        far_opt[j * 128 : (j + 1) * 128, :] = operator[j * 128 : (j + 1) * 128].T.astype(BF16)
    split = n_far * 128
    near_op = near_w[...].reshape(near_wt.shape)
    potential[...] = dot(picked[:, :split], far_op[...]) + dot(picked[:, split:], near_op)
    gradient[...] = dot(collected[:, :split], far_opt[...]) + dot(collected[:, split:], near_wt[...])


def fall_kernel(*refs):
    sources, (potential, gradient), rest = refs[:9], refs[9:11], refs[11:]
    gathered, coarse_list, merge, split, far_w, to_m, to_v, near_pot, near_grad, sems, fall, adj_fall = rest
    fetch = Fetch(sources, rest[:9], sems)
    k = merge.shape[2]
    slots, boxes = coarse_list.shape
    box, child = here() // 8, lax.rem(here(), 8)
    fetch.wait(0, 1, 2)

    def children(c, first):
        at = [gathered[pl.ds(PAIR * c + first + i, boxes, stride=PAIR * 8), :] for i in range(2)]
        return jnp.concatenate(at, axis=1).astype(BF16)

    moments = jnp.concatenate([children(c, 0) for c in range(8)], axis=1)
    coarse_m = dot(moments, merge[...].reshape(8 * k, k)).astype(BF16)
    fetch.wait(3)
    coarse_a = jnp.zeros((boxes, k), F32)
    for c in range(8):
        coarse_a += dot(children(c, 2), split[c], NT)
    coarse_a = coarse_a.astype(BF16)
    listed = coarse_list[...]
    across = lax.broadcasted_iota(jnp.int32, listed.shape, 1)
    named = jnp.sum(jnp.where(across == box, listed, 0), axis=1, keepdims=True)
    picked = dot(jnp.where(across == named, 1.0, 0.0).astype(BF16), coarse_m)
    collected = dot(jnp.where(listed == box, 1.0, 0.0).astype(BF16), coarse_a).astype(BF16)
    picked = jnp.concatenate([picked[j : j + 1, :] for j in range(slots)], axis=1).astype(BF16)
    fetch.wait(4)
    operators = far_w[...].reshape(slots * k, k)
    top = dot(picked, operators).astype(BF16)
    spread = dot(collected, operators, NT)
    adj_top = spread[:1, :k]
    for j in range(1, slots):
        adj_top += spread[j : j + 1, j * k : (j + 1) * k]
    adj_top = adj_top.astype(BF16)
    put_rows(fall, pl.ds(0, 1), rounded(dot(top, split[child])))
    put_rows(adj_fall, pl.ds(0, 1), rounded(dot(adj_top, merge[child], NT)))
    rows = 1
    while rows < fall.shape[1]:
        parents = get_rows(fall, pl.ds(0, rows)).astype(BF16)
        adj_parents = get_rows(adj_fall, pl.ds(0, rows)).astype(BF16)
        adj_spread = rounded(dot(adj_parents, merge[...].reshape(8 * k, k), NT))
        for c in range(8):
            below = pl.ds(c, rows, stride=8) if rows > 1 else pl.ds(c, 1)
            put_rows(fall, below, rounded(dot(parents, split[c])))
            put_rows(adj_fall, below, adj_spread[:, c * k : (c + 1) * k])
        rows *= 8
    fetch.wait(5, 6, 7, 8)
    potential[...] = dot(get_rows(fall, pl.ds(0, rows)).astype(BF16), to_v[...]) + near_pot[...]
    gradient[...] = dot(get_rows(adj_fall, pl.ds(0, rows)).astype(BF16), to_m[...], NT) + near_grad[...]


def near_far_call(far, near, dens, cot, recv_e, recv_o, to_m, to_v, far_w, near_w):
    rows = dens.shape[0]
    k = to_m.shape[1]
    padded = recv_e.shape[0] - 2 * HW
    slots = far.shape[0] + near.shape[0]
    operands = (recv_e, recv_o, far, near, dens, cot, near_w, to_m, to_v, far_w)
    return pl.pallas_call(
        near_far_kernel,
        out_shape=[jax.ShapeDtypeStruct((rows, 128), F32)] * 2,
        in_specs=anywhere(10),
        out_specs=in_vmem(2),
        scratch_shapes=held(*operands)
        + [
            pltpu.VMEM((rows // TILE, TILE, 256), BF16),
            pltpu.VMEM((2 * HW, 256), BF16),
            pltpu.VMEM((padded, rows), F32),
            pltpu.VMEM((padded, 2 * HW), F32),
            pltpu.VMEM((rows, 128), F32),
            pltpu.VMEM((rows, slots * 128), BF16),
            pltpu.VMEM((rows, slots * 128), BF16),
            pltpu.VMEM((near.shape[0] * 128, 128), BF16),
            pltpu.VMEM((far.shape[0] * 128, k), BF16),
            pltpu.VMEM((far.shape[0] * 128, 128), BF16),
            pltpu.VMEM((far.shape[0] * 128, 128), BF16),
        ],
        compiler_params=pltpu.CompilerParams(vmem_limit_bytes=64 << 20),
        cost_estimate=pl.CostEstimate(flops=20 * 10**9, bytes_accessed=5 << 20, transcendentals=0),
        name="near_far",
    )(*operands)


def climb_call(dens, cot, far, near, to_m, to_v, merge, split, count, rim_shape):
    k = to_m.shape[1]
    chain = pltpu.VMEM((k // 128, dens.shape[0], 128), F32)
    operands = (dens, cot, far, near, to_m, to_v, merge, split)
    return pl.pallas_call(
        climb_kernel,
        out_shape=[
            jax.ShapeDtypeStruct((count * 8, 128), F32),
            rim_shape,
            rim_shape,
            jax.ShapeDtypeStruct((8, k, k), BF16),
        ],
        in_specs=anywhere(8),
        out_specs=in_vmem(4),
        scratch_shapes=held(*operands) + [chain, chain, pltpu.VMEM((k // 128, 8 * k, 128), F32)],
        compiler_params=pltpu.CompilerParams(vmem_limit_bytes=64 << 20),
        name="climb",
    )(*operands)


def fall_call(gathered, coarse_list, merge, split, far_w, to_m, to_v, near_pot, near_grad):
    rows = near_pot.shape[0]
    chain = pltpu.VMEM((merge.shape[2] // 128, rows, 128), F32)
    operands = (gathered, coarse_list, merge, split, far_w, to_m, to_v, near_pot, near_grad)
    return pl.pallas_call(
        fall_kernel,
        out_shape=[jax.ShapeDtypeStruct((rows, 128), F32)] * 2,
        in_specs=anywhere(9),
        out_specs=in_vmem(2),
        scratch_shapes=held(*operands) + [chain, chain],
        compiler_params=pltpu.CompilerParams(vmem_limit_bytes=64 << 20),
        name="fall",
    )(*operands)


def per_device(
    densities, cotangents, far_list, near_list, coarse_list,
    to_moments, merge_moments, far_translate, local_split, to_values, near_blocks,
):
    rows = densities.shape[0]
    k = to_moments.shape[1]
    count = lax.axis_size(AXES)
    slots = far_list.shape[0] + near_list.shape[0]
    rim_shape = jax.ShapeDtypeStruct((2 * HW + -(-slots // 16) * 16, 128), BF16)
    row, far_rim, near_rim, split = climb_call(
        densities, cotangents, far_list, near_list, to_moments, to_values, merge_moments, local_split,
        count, rim_shape,
    )
    pairs = [(i, i + 1) for i in range(1, count - 1, 2)]
    recv_o = lax.ppermute(far_rim, AXES, pairs + [(b, a) for a, b in pairs])
    recv_e = lax.ppermute(near_rim, AXES, [(i, i ^ 1) for i in range(count)])
    gathered = lax.all_to_all(row, AXES, 0, 0, tiled=True)
    sums = near_far_call(
        far_list, near_list, densities, cotangents, recv_e, recv_o,
        to_moments, to_values, far_translate, near_blocks,
    )
    return fall_call(
        gathered, coarse_list, merge_moments, split, far_translate, to_moments, to_values, *sums,
    )


def solution(mesh):
    rows = P(AXES, None)
    lists = P(None, AXES)
    return jax.shard_map(
        per_device,
        mesh=mesh,
        in_specs=(rows, rows, lists, lists) + (P(),) * 7,
        out_specs=(rows, rows),
        check_vma=False,
    )
```

```python
import functools

import jax
import jax.numpy as jnp
from jax import lax
from jax.experimental import pallas as pl
from jax.experimental.pallas import tpu as pltpu
from jax.sharding import PartitionSpec as P

HW = 128
TILE = 256
ROWS = 4
AXES = ("coarse", "leaf")
F32 = jnp.float32
BF16 = jnp.bfloat16
NN = (((1,), (0,)), ((), ()))
NT = (((1,), (1,)), ((), ()))


def dot(a, b, dims=NN):
    return lax.dot_general(a, b, dims, preferred_element_type=F32)


def rounded(x):
    return x.astype(BF16).astype(F32)


def anywhere(count):
    return [pl.BlockSpec(memory_space=pl.ANY)] * count


def in_vmem(count):
    return [pl.BlockSpec(memory_space=pltpu.VMEM)] * count


def held(*arrays):
    return [pltpu.VMEM(a.shape, a.dtype) for a in arrays] + [pltpu.SemaphoreType.DMA((len(arrays),))]


class Fetch:
    def __init__(self, sources, targets, sems):
        self.copies = [
            pltpu.make_async_copy(s, t, sems.at[i]) for i, (s, t) in enumerate(zip(sources, targets))
        ]
        for copy in self.copies:
            copy.start()

    def wait(self, *which):
        for i in which:
            self.copies[i].wait()


def get_rows(ref, at):
    return jnp.concatenate([ref[h, at, :] for h in range(ref.shape[0])], axis=1)


def put_rows(ref, at, x):
    for h in range(ref.shape[0]):
        ref[h, at, :] = x[:, h * 128 : (h + 1) * 128]


def here():
    return lax.axis_index(AXES)


def rim(last, dens, cot, far, near, out):
    rows = dens.shape[0]
    pad = out.shape[0] - 2 * HW - far.shape[0] - near.shape[0]
    ends = []
    for at in (slice(rows - HW, rows), slice(0, HW)):
        lists = [far[:, at].astype(F32), near[:, at].astype(F32), jnp.full((pad, HW), -1.0, F32)]
        ends.append(jnp.concatenate(lists, axis=0).astype(BF16))
    out[:HW, :] = jnp.where(last, dens[rows - HW :, :], dens[:HW, :])
    out[HW : 2 * HW, :] = jnp.where(last, cot[rows - HW :, :], cot[:HW, :])
    out[2 * HW :, :] = jnp.where(last, ends[0], ends[1])


def climb_kernel(*refs):
    sources, (out, far_rim, near_rim, split_by_child), rest = refs[:8], refs[8:12], refs[12:]
    dens, cot, to_m, to_v, merge, split, far, near, sems, mom, adj, wide = rest
    fetch = Fetch(sources, rest[:8], sems)
    rows = dens.shape[0]
    k = to_m.shape[1]
    odd = lax.rem(here(), 2) == 1
    child = lax.rem(here(), 8)
    fetch.wait(0, 2)
    put_rows(mom, pl.ds(0, rows), rounded(dot(dens[...], to_m[...])))
    fetch.wait(1, 3)
    put_rows(adj, pl.ds(0, rows), rounded(dot(cot[...], to_v[...], NT)))
    fetch.wait(6, 7)
    rim(odd, dens, cot, far, near, far_rim)
    rim(jnp.logical_not(odd), dens, cot, far, near, near_rim)
    fetch.wait(4, 5)
    for h in range(2):
        wide[h] = split[:, :, h * 128 : (h + 1) * 128].astype(F32).reshape(8 * k, 128)
    for c in range(8):
        split_by_child[c] = get_rows(wide, pl.ds(c, k, stride=8)).astype(BF16)
    while rows > 1:
        rows //= 8
        adj_up = jnp.zeros((rows, k), F32)
        children = [pl.ds(c, rows, stride=8) if rows > 1 else pl.ds(c, 1) for c in range(8)]
        up = jnp.concatenate([get_rows(mom, at) for at in children], axis=1).astype(BF16)
        up = dot(up, merge[...].reshape(8 * k, k))
        for c, at in enumerate(children):
            adj_up += dot(get_rows(adj, at).astype(BF16), split_by_child[c], NT)
        put_rows(mom, pl.ds(0, rows), rounded(up))
        put_rows(adj, pl.ds(0, rows), rounded(adj_up))
    up = dot(up.astype(BF16), merge[child])
    adj_up = dot(adj_up.astype(BF16), split_by_child[child], NT)
    row = jnp.concatenate([x[:, h * 128 : (h + 1) * 128] for x in (up, adj_up) for h in range(2)], axis=0)
    row = jnp.concatenate([row, row], axis=0)
    out[...] = jnp.broadcast_to(row[None], (out.shape[0] // 8, 8, 128)).reshape(out.shape)


def near_far_kernel(*refs):
    sources, (potential, gradient), rest = refs[:10], refs[10:12], refs[12:]
    far, near, recv_e, recv_o, dens, cot, near_w, to_m, to_v, far_w, sems = rest[:11]
    dens_pair, cot_rim, row_place, rim_place, col_targets, picked, collected = rest[11:18]
    near_wt, far_half, far_op, far_opt = rest[18:]
    fetch = Fetch(sources, rest[:10], sems)
    rows = dens.shape[0]
    blocks = rows // TILE
    n_far, n_near = far.shape[0], near.shape[0]
    slots = n_far + n_near
    padded = row_place.shape[0]
    fetch.wait(0, 1)
    listed = jnp.concatenate(
        [far[...].astype(F32), near[...].astype(F32), jnp.full((128 - slots, rows), -1.0, F32)], axis=0
    )
    place = (lax.broadcasted_iota(jnp.int32, listed.shape, 1) % TILE).astype(F32)
    listed = jnp.where(listed >= 0, listed + place, -1.0)
    col_targets[...] = listed.T
    listed = listed[:padded]
    row_place[...] = jnp.where(listed >= TILE, listed - TILE, listed)
    fetch.wait(2, 3, 4, 5)
    odd = lax.rem(here(), 2) == 1
    first, second = recv_e[...], recv_o[...]
    left = jnp.where(odd, first, second)
    right = jnp.where(odd, second, first)
    dens_wide = [left[:HW]] + [dens[i * HW : (i + 1) * HW, :] for i in range(rows // HW)] + [right[:HW]]
    for p in range(blocks):
        for i in range(4):
            at = slice((i % 2) * HW, (i % 2 + 1) * HW)
            dens_pair[p, at, (i // 2) * 128 : (i // 2 + 1) * 128] = dens_wide[2 * p + i]
    cot_rim[...] = jnp.zeros(cot_rim.shape, BF16)
    cot_rim[:HW, :128] = left[HW : 2 * HW]
    cot_rim[HW:, 128:] = right[HW : 2 * HW]
    listed = jnp.concatenate([left[2 * HW :].astype(F32), right[2 * HW :].astype(F32)], axis=1)
    lane = lax.broadcasted_iota(jnp.int32, listed.shape, 1)
    place = jnp.where(lane < HW, lane - TILE, lane - HW).astype(F32)
    rim_place[...] = jnp.where(listed >= 0, listed + place, -1.0)

    lane = lax.broadcasted_iota(jnp.int32, (TILE, 128), 1).astype(F32)
    lanes = [lane.astype(BF16), (lane + 128.0).astype(BF16)]
    down = lax.broadcasted_iota(jnp.int32, (TILE, TILE), 0).astype(F32).astype(BF16)
    one = jnp.ones((), BF16)
    zero = jnp.zeros((), BF16)

    def step(slot):
        at = pl.ds(pl.multiple_of(slot * 128, 128), 128)
        parts = []
        for p in range(blocks):
            own = slice(p * TILE, (p + 1) * TILE)
            column = col_targets[own, :]
            column = jnp.take_along_axis(column, jnp.full(column.shape, slot, jnp.int32), axis=1)
            upper = column >= TILE
            place = jnp.where(upper, column - TILE, column).astype(BF16)
            table = jnp.concatenate([jnp.where(c == place, one, zero) for c in lanes], axis=1)
            both = dot(table, dens_pair[p])
            picked[own, at] = jnp.where(upper, both[:, 128:], both[:, :128]).astype(BF16)
            upper = column.astype(BF16) >= jnp.full((), TILE, BF16)
            values = cot[own, :]
            halves = [jnp.where(upper, zero, values), jnp.where(upper, values, zero)]
            entry = jnp.broadcast_to(row_place[pl.ds(slot, 1), own], (TILE, TILE)).astype(BF16)
            parts.append(dot(jnp.where(down == entry, one, zero), jnp.concatenate(halves, axis=1)))
        entry = jnp.broadcast_to(rim_place[pl.ds(slot, 1), :], (HW, TILE)).astype(BF16)
        rim = dot(jnp.where(down[:HW] == entry, one, zero), cot_rim[...])
        collected[:HW, at] = (parts[0][HW:, :128] + rim[:, :128]).astype(BF16)
        for p in range(blocks - 1):
            own = slice(HW + p * TILE, HW + (p + 1) * TILE)
            collected[own, at] = (parts[p][:, 128:] + parts[p + 1][:, :128]).astype(BF16)
        collected[rows - HW :, at] = (parts[-1][:HW, 128:] + rim[:, 128:]).astype(BF16)

    @pl.loop(0, n_far, unroll=16)
    def _(j):
        step(j)

    fetch.wait(6)

    @pl.loop(0, n_near, unroll=27)
    def _(j):
        step(j + n_far)
        near_wt[pl.ds(pl.multiple_of(j * 128, 128), 128), :] = near_w[j].T

    fetch.wait(7, 8, 9)
    for j in range(n_far):
        far_half[j * 128 : (j + 1) * 128, :] = dot(to_m[...], far_w[j]).astype(BF16)
    operator = dot(far_half[...], to_v[...])
    far_op[...] = operator.astype(BF16)
    for j in range(n_far):
        far_opt[j * 128 : (j + 1) * 128, :] = operator[j * 128 : (j + 1) * 128].T.astype(BF16)
    split = n_far * 128
    near_op = near_w[...].reshape(near_wt.shape)
    potential[...] = dot(picked[:, :split], far_op[...]) + dot(picked[:, split:], near_op)
    gradient[...] = dot(collected[:, :split], far_opt[...]) + dot(collected[:, split:], near_wt[...])


def fall_kernel(*refs):
    sources, (potential, gradient), rest = refs[:9], refs[9:11], refs[11:]
    gathered, coarse_list, far_w, merge, split, to_m, to_v, near_pot, near_grad, sems, fall, adj_fall = rest
    fetch = Fetch(sources, rest[:9], sems)
    k = merge.shape[2]
    slots, boxes = coarse_list.shape
    box, child = here() // 8, lax.rem(here(), 8)
    fetch.wait(0, 1)
    sums = []
    for i in range(ROWS):
        parts = [gathered[pl.ds(ROWS * c + i, boxes, stride=ROWS * 8), :] for c in range(8)]
        sums.append(functools.reduce(jnp.add, parts))
    coarse_m = jnp.concatenate(sums[:2], axis=1).astype(BF16)
    coarse_a = jnp.concatenate(sums[2:], axis=1).astype(BF16)
    listed = coarse_list[...]
    across = lax.broadcasted_iota(jnp.int32, listed.shape, 1)
    named = jnp.sum(jnp.where(across == box, listed, 0), axis=1, keepdims=True)
    picked = dot(jnp.where(across == named, 1.0, 0.0).astype(BF16), coarse_m)
    collected = dot(jnp.where(listed == box, 1.0, 0.0).astype(BF16), coarse_a).astype(BF16)
    picked = jnp.concatenate([picked[j : j + 1, :] for j in range(slots)], axis=1).astype(BF16)
    fetch.wait(2)
    operators = far_w[...].reshape(slots * k, k)
    top = dot(picked, operators).astype(BF16)
    spread = dot(collected, operators, NT)
    adj_top = spread[:1, :k]
    for j in range(1, slots):
        adj_top += spread[j : j + 1, j * k : (j + 1) * k]
    adj_top = adj_top.astype(BF16)
    fetch.wait(3, 4)
    put_rows(fall, pl.ds(0, 1), rounded(dot(top, split[child])))
    put_rows(adj_fall, pl.ds(0, 1), rounded(dot(adj_top, merge[child], NT)))
    rows = 1
    while rows < fall.shape[1]:
        parents = get_rows(fall, pl.ds(0, rows)).astype(BF16)
        adj_parents = get_rows(adj_fall, pl.ds(0, rows)).astype(BF16)
        adj_spread = rounded(dot(adj_parents, merge[...].reshape(8 * k, k), NT))
        for c in range(8):
            below = pl.ds(c, rows, stride=8) if rows > 1 else pl.ds(c, 1)
            put_rows(fall, below, rounded(dot(parents, split[c])))
            put_rows(adj_fall, below, adj_spread[:, c * k : (c + 1) * k])
        rows *= 8
    fetch.wait(5, 6, 7, 8)
    potential[...] = dot(get_rows(fall, pl.ds(0, rows)).astype(BF16), to_v[...]) + near_pot[...]
    gradient[...] = dot(get_rows(adj_fall, pl.ds(0, rows)).astype(BF16), to_m[...], NT) + near_grad[...]


def near_far_call(far, near, dens, cot, recv_e, recv_o, to_m, to_v, far_w, near_w):
    rows = dens.shape[0]
    k = to_m.shape[1]
    padded = recv_e.shape[0] - 2 * HW
    slots = far.shape[0] + near.shape[0]
    operands = (far, near, recv_e, recv_o, dens, cot, near_w, to_m, to_v, far_w)
    return pl.pallas_call(
        near_far_kernel,
        out_shape=[jax.ShapeDtypeStruct((rows, 128), F32)] * 2,
        in_specs=anywhere(10),
        out_specs=in_vmem(2),
        scratch_shapes=held(*operands)
        + [
            pltpu.VMEM((rows // TILE, TILE, 256), BF16),
            pltpu.VMEM((2 * HW, 256), BF16),
            pltpu.VMEM((padded, rows), F32),
            pltpu.VMEM((padded, 2 * HW), F32),
            pltpu.VMEM((rows, 128), F32),
            pltpu.VMEM((rows, slots * 128), BF16),
            pltpu.VMEM((rows, slots * 128), BF16),
            pltpu.VMEM((near.shape[0] * 128, 128), BF16),
            pltpu.VMEM((far.shape[0] * 128, k), BF16),
            pltpu.VMEM((far.shape[0] * 128, 128), BF16),
            pltpu.VMEM((far.shape[0] * 128, 128), BF16),
        ],
        compiler_params=pltpu.CompilerParams(vmem_limit_bytes=64 << 20),
        cost_estimate=pl.CostEstimate(flops=20 * 10**9, bytes_accessed=5 << 20, transcendentals=0),
        name="near_far",
    )(*operands)


def climb_call(dens, cot, far, near, to_m, to_v, merge, split, count, rim_shape):
    k = to_m.shape[1]
    chain = pltpu.VMEM((k // 128, dens.shape[0], 128), F32)
    operands = (dens, cot, to_m, to_v, merge, split, far, near)
    return pl.pallas_call(
        climb_kernel,
        out_shape=[
            jax.ShapeDtypeStruct((count * ROWS, 128), F32),
            rim_shape,
            rim_shape,
            jax.ShapeDtypeStruct((8, k, k), BF16),
        ],
        in_specs=anywhere(8),
        out_specs=in_vmem(4),
        scratch_shapes=held(*operands) + [chain, chain, pltpu.VMEM((k // 128, 8 * k, 128), F32)],
        compiler_params=pltpu.CompilerParams(vmem_limit_bytes=64 << 20),
        name="climb",
    )(*operands)


def fall_call(gathered, coarse_list, merge, split, far_w, to_m, to_v, near_pot, near_grad):
    rows = near_pot.shape[0]
    chain = pltpu.VMEM((merge.shape[2] // 128, rows, 128), F32)
    operands = (gathered, coarse_list, far_w, merge, split, to_m, to_v, near_pot, near_grad)
    return pl.pallas_call(
        fall_kernel,
        out_shape=[jax.ShapeDtypeStruct((rows, 128), F32)] * 2,
        in_specs=anywhere(9),
        out_specs=in_vmem(2),
        scratch_shapes=held(*operands) + [chain, chain],
        compiler_params=pltpu.CompilerParams(vmem_limit_bytes=64 << 20),
        name="fall",
    )(*operands)


def per_device(
    densities, cotangents, far_list, near_list, coarse_list,
    to_moments, merge_moments, far_translate, local_split, to_values, near_blocks,
):
    rows = densities.shape[0]
    k = to_moments.shape[1]
    count = lax.axis_size(AXES)
    slots = far_list.shape[0] + near_list.shape[0]
    rim_shape = jax.ShapeDtypeStruct((2 * HW + -(-slots // 16) * 16, 128), BF16)
    row, far_rim, near_rim, split = climb_call(
        densities, cotangents, far_list, near_list, to_moments, to_values, merge_moments, local_split,
        count, rim_shape,
    )
    pairs = [(i, i + 1) for i in range(1, count - 1, 2)]
    recv_o = lax.ppermute(far_rim, AXES, pairs + [(b, a) for a, b in pairs])
    recv_e = lax.ppermute(near_rim, AXES, [(i, i ^ 1) for i in range(count)])
    gathered = lax.all_to_all(row, AXES, 0, 0, tiled=True)
    sums = near_far_call(
        far_list, near_list, densities, cotangents, recv_e, recv_o,
        to_moments, to_values, far_translate, near_blocks,
    )
    return fall_call(
        gathered, coarse_list, merge_moments, split, far_translate, to_moments, to_values, *sums,
    )


def solution(mesh):
    rows = P(AXES, None)
    lists = P(None, AXES)
    return jax.shard_map(
        per_device,
        mesh=mesh,
        in_specs=(rows, rows, lists, lists) + (P(),) * 7,
        out_specs=(rows, rows),
        check_vma=False,
    )
```

```python
import functools

import jax
import jax.numpy as jnp
from jax import lax
from jax.experimental import pallas as pl
from jax.experimental.pallas import tpu as pltpu
from jax.sharding import PartitionSpec as P

HW = 128
TILE = 256
ROWS = 4
AXES = ("coarse", "leaf")
F32 = jnp.float32
BF16 = jnp.bfloat16
NN = (((1,), (0,)), ((), ()))
NT = (((1,), (1,)), ((), ()))


def dot(a, b, dims=NN):
    return lax.dot_general(a, b, dims, preferred_element_type=F32)


def rounded(x):
    return x.astype(BF16).astype(F32)


def anywhere(count):
    return [pl.BlockSpec(memory_space=pl.ANY)] * count


def in_vmem(count):
    return [pl.BlockSpec(memory_space=pltpu.VMEM)] * count


def held(*arrays):
    return [pltpu.VMEM(a.shape, a.dtype) for a in arrays] + [pltpu.SemaphoreType.DMA((len(arrays),))]


class Fetch:
    def __init__(self, sources, targets, sems):
        self.copies = [
            pltpu.make_async_copy(s, t, sems.at[i]) for i, (s, t) in enumerate(zip(sources, targets))
        ]
        for copy in self.copies:
            copy.start()

    def wait(self, *which):
        for i in which:
            self.copies[i].wait()


def get_rows(ref, at):
    return jnp.concatenate([ref[h, at, :] for h in range(ref.shape[0])], axis=1)


def put_rows(ref, at, x):
    for h in range(ref.shape[0]):
        ref[h, at, :] = x[:, h * 128 : (h + 1) * 128]


def here():
    return lax.axis_index(AXES)


def rim(last, dens, cot, far, near, out):
    rows = dens.shape[0]
    pad = out.shape[0] - 2 * HW - far.shape[0] - near.shape[0]
    ends = []
    for at in (slice(rows - HW, rows), slice(0, HW)):
        lists = [far[:, at].astype(F32), near[:, at].astype(F32), jnp.full((pad, HW), -1.0, F32)]
        ends.append(jnp.concatenate(lists, axis=0).astype(BF16))
    out[:HW, :] = jnp.where(last, dens[rows - HW :, :], dens[:HW, :])
    out[HW : 2 * HW, :] = jnp.where(last, cot[rows - HW :, :], cot[:HW, :])
    out[2 * HW :, :] = jnp.where(last, ends[0], ends[1])


def climb_kernel(*refs):
    sources, (out, far_rim, near_rim, split_by_child), rest = refs[:8], refs[8:12], refs[12:]
    dens, cot, to_m, to_v, merge, split, far, near, sems, mom, adj, wide = rest
    fetch = Fetch(sources, rest[:8], sems)
    rows = dens.shape[0]
    k = to_m.shape[1]
    odd = lax.rem(here(), 2) == 1
    child = lax.rem(here(), 8)
    fetch.wait(0, 2)
    put_rows(mom, pl.ds(0, rows), rounded(dot(dens[...], to_m[...])))
    fetch.wait(1, 3)
    put_rows(adj, pl.ds(0, rows), rounded(dot(cot[...], to_v[...], NT)))
    fetch.wait(6, 7)
    rim(odd, dens, cot, far, near, far_rim)
    rim(jnp.logical_not(odd), dens, cot, far, near, near_rim)
    fetch.wait(4, 5)
    for h in range(2):
        wide[h] = split[:, :, h * 128 : (h + 1) * 128].astype(F32).reshape(8 * k, 128)
    for c in range(8):
        split_by_child[c] = get_rows(wide, pl.ds(c, k, stride=8)).astype(BF16)
    while rows > 1:
        rows //= 8
        adj_up = jnp.zeros((rows, k), F32)
        children = [pl.ds(c, rows, stride=8) if rows > 1 else pl.ds(c, 1) for c in range(8)]
        up = jnp.concatenate([get_rows(mom, at) for at in children], axis=1).astype(BF16)
        up = dot(up, merge[...].reshape(8 * k, k))
        for c, at in enumerate(children):
            adj_up += dot(get_rows(adj, at).astype(BF16), split_by_child[c], NT)
        put_rows(mom, pl.ds(0, rows), rounded(up))
        put_rows(adj, pl.ds(0, rows), rounded(adj_up))
    up = dot(up.astype(BF16), merge[child])
    adj_up = dot(adj_up.astype(BF16), split_by_child[child], NT)
    row = jnp.concatenate([x[:, h * 128 : (h + 1) * 128] for x in (up, adj_up) for h in range(2)], axis=0)
    row = jnp.concatenate([row, row], axis=0)
    out[...] = jnp.broadcast_to(row[None], (out.shape[0] // 8, 8, 128)).reshape(out.shape)


def near_far_kernel(*refs):
    sources, (potential, gradient), rest = refs[:10], refs[10:12], refs[12:]
    far, near, recv_e, recv_o, dens, cot, op, to_m, to_v, far_w, sems = rest[:11]
    dens_pair, cot_rim, row_place, rim_place, col_targets, picked, collected = rest[11:18]
    far_half, opt = rest[18:]
    first = far.shape[0]
    targets = list(rest[:10])
    targets[6] = near_w = op.at[pl.ds(first, near.shape[0])]
    fetch = Fetch(sources, targets, sems)
    rows = dens.shape[0]
    blocks = rows // TILE
    n_far, n_near = far.shape[0], near.shape[0]
    slots = n_far + n_near
    padded = row_place.shape[0]
    fetch.wait(0, 1)
    listed = jnp.concatenate(
        [far[...].astype(F32), near[...].astype(F32), jnp.full((128 - slots, rows), -1.0, F32)], axis=0
    )
    place = (lax.broadcasted_iota(jnp.int32, listed.shape, 1) % TILE).astype(F32)
    listed = jnp.where(listed >= 0, listed + place, -1.0)
    coded = jnp.where(listed >= TILE, TILE - 1 - listed, listed)
    col_targets[...] = jnp.where(listed >= 0, coded, -1000.0).T
    listed = listed[:padded]
    row_place[...] = jnp.where(listed >= TILE, listed - TILE, listed)
    fetch.wait(2, 3, 4, 5)
    odd = lax.rem(here(), 2) == 1
    first, second = recv_e[...], recv_o[...]
    left = jnp.where(odd, first, second)
    right = jnp.where(odd, second, first)
    dens_wide = [left[:HW]] + [dens[i * HW : (i + 1) * HW, :] for i in range(rows // HW)] + [right[:HW]]
    for p in range(blocks):
        for i in range(4):
            at = slice((i % 2) * HW, (i % 2 + 1) * HW)
            dens_pair[p, at, (i // 2) * 128 : (i // 2 + 1) * 128] = dens_wide[2 * p + i]
    cot_rim[...] = jnp.zeros(cot_rim.shape, BF16)
    cot_rim[:HW, :128] = left[HW : 2 * HW]
    cot_rim[HW:, 128:] = right[HW : 2 * HW]
    listed = jnp.concatenate([left[2 * HW :].astype(F32), right[2 * HW :].astype(F32)], axis=1)
    lane = lax.broadcasted_iota(jnp.int32, listed.shape, 1)
    place = jnp.where(lane < HW, lane - TILE, lane - HW).astype(F32)
    rim_place[...] = jnp.where(listed >= 0, listed + place, -1.0)

    lane = lax.broadcasted_iota(jnp.int32, (TILE, 128), 1).astype(F32)
    lanes = [lane.astype(BF16), (lane + 128.0).astype(BF16)]
    down = lax.broadcasted_iota(jnp.int32, (TILE, TILE), 0).astype(F32).astype(BF16)
    one = jnp.ones((), BF16)
    zero = jnp.zeros((), BF16)

    def step(slot):
        at = pl.ds(pl.multiple_of(slot * 128, 128), 128)
        parts = []
        for p in range(blocks):
            own = slice(p * TILE, (p + 1) * TILE)
            column = col_targets[own, :]
            column = jnp.take_along_axis(column, jnp.full(column.shape, slot, jnp.int32), axis=1)
            column = column.astype(BF16)
            upper = column < zero
            place = jnp.where(upper, -one - column, column)
            table = jnp.concatenate([jnp.where(c == place, one, zero) for c in lanes], axis=1)
            both = dot(table, dens_pair[p]).astype(BF16)
            picked[own, at] = jnp.where(upper, both[:, 128:], both[:, :128])
            values = cot[own, :]
            halves = [jnp.where(upper, zero, values), jnp.where(upper, values, zero)]
            entry = jnp.broadcast_to(row_place[pl.ds(slot, 1), own], (TILE, TILE)).astype(BF16)
            parts.append(dot(jnp.where(down == entry, one, zero), jnp.concatenate(halves, axis=1)))
        entry = jnp.broadcast_to(rim_place[pl.ds(slot, 1), :], (HW, TILE)).astype(BF16)
        rim = dot(jnp.where(down[:HW] == entry, one, zero), cot_rim[...])
        collected[:HW, at] = (parts[0][HW:, :128] + rim[:, :128]).astype(BF16)
        for p in range(blocks - 1):
            own = slice(HW + p * TILE, HW + (p + 1) * TILE)
            collected[own, at] = (parts[p][:, 128:] + parts[p + 1][:, :128]).astype(BF16)
        collected[rows - HW :, at] = (parts[-1][:HW, 128:] + rim[:, 128:]).astype(BF16)

    @pl.loop(0, n_far, unroll=16)
    def _(j):
        step(j)

    fetch.wait(6, 7, 8, 9)

    @pl.loop(0, n_near, unroll=27)
    def _(j):
        step(j + n_far)
        opt[pl.ds(pl.multiple_of((j + n_far) * 128, 128), 128), :] = op[j + n_far].T

    for j in range(n_far):
        far_half[j * 128 : (j + 1) * 128, :] = dot(to_m[...], far_w[j]).astype(BF16)
    operator = dot(far_half[...], to_v[...])
    for j in range(n_far):
        part = operator[j * 128 : (j + 1) * 128]
        op[j] = part.astype(BF16)
        opt[j * 128 : (j + 1) * 128, :] = part.T.astype(BF16)
    potential[...] = dot(picked[...], op[...].reshape(opt.shape))
    gradient[...] = dot(collected[...], opt[...])


def fall_kernel(*refs):
    sources, (potential, gradient), rest = refs[:9], refs[9:11], refs[11:]
    gathered, coarse_list, far_w, merge, split, to_m, to_v, near_pot, near_grad, sems, fall, adj_fall = rest
    fetch = Fetch(sources, rest[:9], sems)
    k = merge.shape[2]
    slots, boxes = coarse_list.shape
    box, child = here() // 8, lax.rem(here(), 8)
    fetch.wait(0, 1)
    sums = []
    for i in range(ROWS):
        parts = [gathered[pl.ds(ROWS * c + i, boxes, stride=ROWS * 8), :] for c in range(8)]
        sums.append(functools.reduce(jnp.add, parts))
    coarse_m = jnp.concatenate(sums[:2], axis=1).astype(BF16)
    coarse_a = jnp.concatenate(sums[2:], axis=1).astype(BF16)
    listed = coarse_list[...]
    across = lax.broadcasted_iota(jnp.int32, listed.shape, 1)
    named = jnp.sum(jnp.where(across == box, listed, 0), axis=1, keepdims=True)
    picked = dot(jnp.where(across == named, 1.0, 0.0).astype(BF16), coarse_m)
    collected = dot(jnp.where(listed == box, 1.0, 0.0).astype(BF16), coarse_a).astype(BF16)
    picked = jnp.concatenate([picked[j : j + 1, :] for j in range(slots)], axis=1).astype(BF16)
    fetch.wait(2)
    operators = far_w[...].reshape(slots * k, k)
    top = dot(picked, operators).astype(BF16)
    spread = dot(collected, operators, NT)
    adj_top = spread[:1, :k]
    for j in range(1, slots):
        adj_top += spread[j : j + 1, j * k : (j + 1) * k]
    adj_top = adj_top.astype(BF16)
    fetch.wait(3, 4)
    put_rows(fall, pl.ds(0, 1), rounded(dot(top, split[child])))
    put_rows(adj_fall, pl.ds(0, 1), rounded(dot(adj_top, merge[child], NT)))
    rows = 1
    while rows < fall.shape[1]:
        parents = get_rows(fall, pl.ds(0, rows)).astype(BF16)
        adj_parents = get_rows(adj_fall, pl.ds(0, rows)).astype(BF16)
        adj_spread = rounded(dot(adj_parents, merge[...].reshape(8 * k, k), NT))
        for c in range(8):
            below = pl.ds(c, rows, stride=8) if rows > 1 else pl.ds(c, 1)
            put_rows(fall, below, rounded(dot(parents, split[c])))
            put_rows(adj_fall, below, adj_spread[:, c * k : (c + 1) * k])
        rows *= 8
    fetch.wait(5, 6, 7, 8)
    potential[...] = dot(get_rows(fall, pl.ds(0, rows)).astype(BF16), to_v[...]) + near_pot[...]
    gradient[...] = dot(get_rows(adj_fall, pl.ds(0, rows)).astype(BF16), to_m[...], NT) + near_grad[...]


def near_far_call(far, near, dens, cot, recv_e, recv_o, to_m, to_v, far_w, near_w):
    rows = dens.shape[0]
    k = to_m.shape[1]
    padded = recv_e.shape[0] - 2 * HW
    slots = far.shape[0] + near.shape[0]
    operands = (far, near, recv_e, recv_o, dens, cot, near_w, to_m, to_v, far_w)
    shapes = list(operands)
    shapes[6] = jax.ShapeDtypeStruct((slots, 128, 128), BF16)
    return pl.pallas_call(
        near_far_kernel,
        out_shape=[jax.ShapeDtypeStruct((rows, 128), F32)] * 2,
        in_specs=anywhere(10),
        out_specs=in_vmem(2),
        scratch_shapes=held(*shapes)
        + [
            pltpu.VMEM((rows // TILE, TILE, 256), BF16),
            pltpu.VMEM((2 * HW, 256), BF16),
            pltpu.VMEM((padded, rows), F32),
            pltpu.VMEM((padded, 2 * HW), F32),
            pltpu.VMEM((rows, 128), F32),
            pltpu.VMEM((rows, slots * 128), BF16),
            pltpu.VMEM((rows, slots * 128), BF16),
            pltpu.VMEM((far.shape[0] * 128, k), BF16),
            pltpu.VMEM((slots * 128, 128), BF16),
        ],
        compiler_params=pltpu.CompilerParams(vmem_limit_bytes=64 << 20),
        cost_estimate=pl.CostEstimate(flops=20 * 10**9, bytes_accessed=5 << 20, transcendentals=0),
        name="near_far",
    )(*operands)


def climb_call(dens, cot, far, near, to_m, to_v, merge, split, count, rim_shape):
    k = to_m.shape[1]
    chain = pltpu.VMEM((k // 128, dens.shape[0], 128), F32)
    operands = (dens, cot, to_m, to_v, merge, split, far, near)
    return pl.pallas_call(
        climb_kernel,
        out_shape=[
            jax.ShapeDtypeStruct((count * ROWS, 128), F32),
            rim_shape,
            rim_shape,
            jax.ShapeDtypeStruct((8, k, k), BF16),
        ],
        in_specs=anywhere(8),
        out_specs=in_vmem(4),
        scratch_shapes=held(*operands) + [chain, chain, pltpu.VMEM((k // 128, 8 * k, 128), F32)],
        compiler_params=pltpu.CompilerParams(vmem_limit_bytes=64 << 20),
        name="climb",
    )(*operands)


def fall_call(gathered, coarse_list, merge, split, far_w, to_m, to_v, near_pot, near_grad):
    rows = near_pot.shape[0]
    chain = pltpu.VMEM((merge.shape[2] // 128, rows, 128), F32)
    operands = (gathered, coarse_list, far_w, merge, split, to_m, to_v, near_pot, near_grad)
    return pl.pallas_call(
        fall_kernel,
        out_shape=[jax.ShapeDtypeStruct((rows, 128), F32)] * 2,
        in_specs=anywhere(9),
        out_specs=in_vmem(2),
        scratch_shapes=held(*operands) + [chain, chain],
        compiler_params=pltpu.CompilerParams(vmem_limit_bytes=64 << 20),
        name="fall",
    )(*operands)


def per_device(
    densities, cotangents, far_list, near_list, coarse_list,
    to_moments, merge_moments, far_translate, local_split, to_values, near_blocks,
):
    rows = densities.shape[0]
    k = to_moments.shape[1]
    count = lax.axis_size(AXES)
    slots = far_list.shape[0] + near_list.shape[0]
    rim_shape = jax.ShapeDtypeStruct((2 * HW + -(-slots // 16) * 16, 128), BF16)
    row, far_rim, near_rim, split = climb_call(
        densities, cotangents, far_list, near_list, to_moments, to_values, merge_moments, local_split,
        count, rim_shape,
    )
    pairs = [(i, i + 1) for i in range(1, count - 1, 2)]
    recv_o = lax.ppermute(far_rim, AXES, pairs + [(b, a) for a, b in pairs])
    recv_e = lax.ppermute(near_rim, AXES, [(i, i ^ 1) for i in range(count)])
    gathered = lax.all_to_all(row, AXES, 0, 0, tiled=True)
    sums = near_far_call(
        far_list, near_list, densities, cotangents, recv_e, recv_o,
        to_moments, to_values, far_translate, near_blocks,
    )
    return fall_call(
        gathered, coarse_list, merge_moments, split, far_translate, to_moments, to_values, *sums,
    )


def solution(mesh):
    rows = P(AXES, None)
    lists = P(None, AXES)
    return jax.shard_map(
        per_device,
        mesh=mesh,
        in_specs=(rows, rows, lists, lists) + (P(),) * 7,
        out_specs=(rows, rows),
        check_vma=False,
    )
```

```python
import functools

import jax
import jax.numpy as jnp
from jax import lax
from jax.experimental import pallas as pl
from jax.experimental.pallas import tpu as pltpu
from jax.sharding import PartitionSpec as P

HW = 128
TILE = 256
ROWS = 4
AXES = ("coarse", "leaf")
F32 = jnp.float32
BF16 = jnp.bfloat16
NN = (((1,), (0,)), ((), ()))
NT = (((1,), (1,)), ((), ()))


def dot(a, b, dims=NN):
    return lax.dot_general(a, b, dims, preferred_element_type=F32)


def rounded(x):
    return x.astype(BF16).astype(F32)


def anywhere(count):
    return [pl.BlockSpec(memory_space=pl.ANY)] * count


def in_vmem(count):
    return [pl.BlockSpec(memory_space=pltpu.VMEM)] * count


def held(*arrays):
    return [pltpu.VMEM(a.shape, a.dtype) for a in arrays] + [pltpu.SemaphoreType.DMA((len(arrays),))]


class Fetch:
    def __init__(self, sources, targets, sems, order=None):
        self.copies = [
            pltpu.make_async_copy(s, t, sems.at[i]) for i, (s, t) in enumerate(zip(sources, targets))
        ]
        for i in order or range(len(self.copies)):
            self.copies[i].start()

    def wait(self, *which):
        for i in which:
            self.copies[i].wait()


def get_rows(ref, at):
    return jnp.concatenate([ref[h, at, :] for h in range(ref.shape[0])], axis=1)


def put_rows(ref, at, x):
    for h in range(ref.shape[0]):
        ref[h, at, :] = x[:, h * 128 : (h + 1) * 128]


def here():
    return lax.axis_index(AXES)


def rim(last, dens, cot, far, near, out):
    rows = dens.shape[0]
    pad = out.shape[0] - 2 * HW - far.shape[0] - near.shape[0]
    ends = []
    for at in (slice(rows - HW, rows), slice(0, HW)):
        lists = [far[:, at].astype(F32), near[:, at].astype(F32), jnp.full((pad, HW), -1.0, F32)]
        ends.append(jnp.concatenate(lists, axis=0).astype(BF16))
    out[:HW, :] = jnp.where(last, dens[rows - HW :, :], dens[:HW, :])
    out[HW : 2 * HW, :] = jnp.where(last, cot[rows - HW :, :], cot[:HW, :])
    out[2 * HW :, :] = jnp.where(last, ends[0], ends[1])


def climb_kernel(*refs):
    sources, (out, far_rim, near_rim, split_by_child), rest = refs[:8], refs[8:12], refs[12:]
    dens, cot, to_m, to_v, merge, split, far, near, sems, mom, adj, wide = rest
    fetch = Fetch(sources, rest[:8], sems)
    rows = dens.shape[0]
    k = to_m.shape[1]
    odd = lax.rem(here(), 2) == 1
    child = lax.rem(here(), 8)
    fetch.wait(0, 2)
    put_rows(mom, pl.ds(0, rows), rounded(dot(dens[...], to_m[...])))
    fetch.wait(1, 3)
    put_rows(adj, pl.ds(0, rows), rounded(dot(cot[...], to_v[...], NT)))
    fetch.wait(6, 7)
    rim(odd, dens, cot, far, near, far_rim)
    rim(jnp.logical_not(odd), dens, cot, far, near, near_rim)
    fetch.wait(4, 5)
    for h in range(2):
        wide[h] = split[:, :, h * 128 : (h + 1) * 128].astype(F32).reshape(8 * k, 128)
    for c in range(8):
        split_by_child[c] = get_rows(wide, pl.ds(c, k, stride=8)).astype(BF16)
    while rows > 1:
        rows //= 8
        adj_up = jnp.zeros((rows, k), F32)
        children = [pl.ds(c, rows, stride=8) if rows > 1 else pl.ds(c, 1) for c in range(8)]
        up = jnp.concatenate([get_rows(mom, at) for at in children], axis=1).astype(BF16)
        up = dot(up, merge[...].reshape(8 * k, k))
        for c, at in enumerate(children):
            adj_up += dot(get_rows(adj, at).astype(BF16), split_by_child[c], NT)
        put_rows(mom, pl.ds(0, rows), rounded(up))
        put_rows(adj, pl.ds(0, rows), rounded(adj_up))
    up = dot(up.astype(BF16), merge[child])
    adj_up = dot(adj_up.astype(BF16), split_by_child[child], NT)
    row = jnp.concatenate([x[:, h * 128 : (h + 1) * 128] for x in (up, adj_up) for h in range(2)], axis=0)
    row = jnp.concatenate([row, row], axis=0)
    out[...] = jnp.broadcast_to(row[None], (out.shape[0] // 8, 8, 128)).reshape(out.shape)


def near_far_kernel(*refs):
    sources, (potential, gradient), rest = refs[:10], refs[10:12], refs[12:]
    far, near, recv_e, recv_o, dens, cot, op, to_m, to_v, far_w, sems = rest[:11]
    dens_pair, cot_rim, row_place, rim_place, col_targets, picked, collected = rest[11:18]
    far_half, opt = rest[18:]
    first = far.shape[0]
    targets = list(rest[:10])
    targets[6] = near_w = op.at[pl.ds(first, near.shape[0])]
    fetch = Fetch(sources, targets, sems)
    rows = dens.shape[0]
    blocks = rows // TILE
    n_far, n_near = far.shape[0], near.shape[0]
    slots = n_far + n_near
    padded = row_place.shape[0]
    fetch.wait(0, 1)
    listed = jnp.concatenate(
        [far[...].astype(F32), near[...].astype(F32), jnp.full((128 - slots, rows), -1.0, F32)], axis=0
    )
    place = (lax.broadcasted_iota(jnp.int32, listed.shape, 1) % TILE).astype(F32)
    listed = jnp.where(listed >= 0, listed + place, -1.0)
    coded = jnp.where(listed >= TILE, TILE - 1 - listed, listed)
    col_targets[...] = jnp.where(listed >= 0, coded, -1000.0).T
    listed = listed[:padded]
    row_place[...] = jnp.where(listed >= TILE, listed - TILE, listed)
    fetch.wait(2, 3, 4, 5)
    odd = lax.rem(here(), 2) == 1
    first, second = recv_e[...], recv_o[...]
    left = jnp.where(odd, first, second)
    right = jnp.where(odd, second, first)
    dens_wide = [left[:HW]] + [dens[i * HW : (i + 1) * HW, :] for i in range(rows // HW)] + [right[:HW]]
    for p in range(blocks):
        for i in range(4):
            at = slice((i % 2) * HW, (i % 2 + 1) * HW)
            dens_pair[p, at, (i // 2) * 128 : (i // 2 + 1) * 128] = dens_wide[2 * p + i]
    cot_rim[...] = jnp.zeros(cot_rim.shape, BF16)
    cot_rim[:HW, :128] = left[HW : 2 * HW]
    cot_rim[HW:, 128:] = right[HW : 2 * HW]
    listed = jnp.concatenate([left[2 * HW :].astype(F32), right[2 * HW :].astype(F32)], axis=1)
    lane = lax.broadcasted_iota(jnp.int32, listed.shape, 1)
    place = jnp.where(lane < HW, lane - TILE, lane - HW).astype(F32)
    rim_place[...] = jnp.where(listed >= 0, listed + place, -1.0)

    lane = lax.broadcasted_iota(jnp.int32, (TILE, 128), 1).astype(F32)
    lanes = [lane.astype(BF16), (lane + 128.0).astype(BF16)]
    down = lax.broadcasted_iota(jnp.int32, (TILE, TILE), 0).astype(F32).astype(BF16)
    one = jnp.ones((), BF16)
    zero = jnp.zeros((), BF16)

    def step(slot):
        at = pl.ds(pl.multiple_of(slot * 128, 128), 128)
        parts = []
        for p in range(blocks):
            own = slice(p * TILE, (p + 1) * TILE)
            column = col_targets[own, :]
            column = jnp.take_along_axis(column, jnp.full(column.shape, slot, jnp.int32), axis=1)
            column = column.astype(BF16)
            upper = column < zero
            place = jnp.where(upper, -one - column, column)
            table = jnp.concatenate([jnp.where(c == place, one, zero) for c in lanes], axis=1)
            both = dot(table, dens_pair[p]).astype(BF16)
            picked[own, at] = jnp.where(upper, both[:, 128:], both[:, :128])
            values = cot[own, :]
            halves = [jnp.where(upper, zero, values), jnp.where(upper, values, zero)]
            entry = jnp.broadcast_to(row_place[pl.ds(slot, 1), own], (TILE, TILE)).astype(BF16)
            parts.append(dot(jnp.where(down == entry, one, zero), jnp.concatenate(halves, axis=1)))
        entry = jnp.broadcast_to(rim_place[pl.ds(slot, 1), :], (HW, TILE)).astype(BF16)
        rim = dot(jnp.where(down[:HW] == entry, one, zero), cot_rim[...])
        collected[:HW, at] = (parts[0][HW:, :128] + rim[:, :128]).astype(BF16)
        for p in range(blocks - 1):
            own = slice(HW + p * TILE, HW + (p + 1) * TILE)
            collected[own, at] = (parts[p][:, 128:] + parts[p + 1][:, :128]).astype(BF16)
        collected[rows - HW :, at] = (parts[-1][:HW, 128:] + rim[:, 128:]).astype(BF16)

    @pl.loop(0, n_far, unroll=16)
    def _(j):
        step(j)

    fetch.wait(6, 7, 8, 9)

    @pl.loop(0, n_near, unroll=27)
    def _(j):
        step(j + n_far)
        opt[pl.ds(pl.multiple_of((j + n_far) * 128, 128), 128), :] = op[j + n_far].T

    for j in range(n_far):
        far_half[j * 128 : (j + 1) * 128, :] = dot(to_m[...], far_w[j]).astype(BF16)
    operator = dot(far_half[...], to_v[...])
    for j in range(n_far):
        part = operator[j * 128 : (j + 1) * 128]
        op[j] = part.astype(BF16)
        opt[j * 128 : (j + 1) * 128, :] = part.T.astype(BF16)
    potential[...] = dot(picked[...], op[...].reshape(opt.shape))
    gradient[...] = dot(collected[...], opt[...])


def fall_kernel(*refs):
    sources, (potential, gradient), rest = refs[:9], refs[9:11], refs[11:]
    gathered, coarse_list, far_w, merge, split, to_m, to_v, near_pot, near_grad, sems, fall, adj_fall = rest
    half = far_w.shape[0] // 2
    sources, targets = list(sources), list(rest[:9])
    for held_by in (sources, targets):
        held_by.append(held_by[2].at[pl.ds(half, half)])
        held_by[2] = held_by[2].at[pl.ds(0, half)]
    fetch = Fetch(sources, targets, sems, (0, 1, 2, 9, 3, 4, 5, 6, 7, 8))
    k = merge.shape[2]
    slots, boxes = coarse_list.shape
    box, child = here() // 8, lax.rem(here(), 8)
    fetch.wait(0, 1)
    sums = []
    for i in range(ROWS):
        parts = [gathered[pl.ds(ROWS * c + i, boxes, stride=ROWS * 8), :] for c in range(8)]
        sums.append(functools.reduce(jnp.add, parts))
    coarse_m = jnp.concatenate(sums[:2], axis=1).astype(BF16)
    coarse_a = jnp.concatenate(sums[2:], axis=1).astype(BF16)
    listed = coarse_list[...]
    across = lax.broadcasted_iota(jnp.int32, listed.shape, 1)
    named = jnp.sum(jnp.where(across == box, listed, 0), axis=1, keepdims=True)
    picked = dot(jnp.where(across == named, 1.0, 0.0).astype(BF16), coarse_m)
    collected = dot(jnp.where(listed == box, 1.0, 0.0).astype(BF16), coarse_a).astype(BF16)
    picked = jnp.concatenate([picked[j : j + 1, :] for j in range(slots)], axis=1).astype(BF16)
    half = slots // 2
    top, adj_top = jnp.zeros((1, k), F32), jnp.zeros((1, k), F32)
    for part, lo in enumerate((0, half)):
        fetch.wait((2, 9)[part])
        operators = far_w[lo : lo + half].reshape(half * k, k)
        top += dot(picked[:, lo * k : (lo + half) * k], operators)
        spread = dot(collected, operators, NT)
        for j in range(half):
            adj_top += spread[lo + j : lo + j + 1, j * k : (j + 1) * k]
    top = top.astype(BF16)
    adj_top = adj_top.astype(BF16)
    fetch.wait(3, 4)
    put_rows(fall, pl.ds(0, 1), rounded(dot(top, split[child])))
    put_rows(adj_fall, pl.ds(0, 1), rounded(dot(adj_top, merge[child], NT)))
    rows = 1
    while rows < fall.shape[1]:
        parents = get_rows(fall, pl.ds(0, rows)).astype(BF16)
        adj_parents = get_rows(adj_fall, pl.ds(0, rows)).astype(BF16)
        adj_spread = rounded(dot(adj_parents, merge[...].reshape(8 * k, k), NT))
        for c in range(8):
            below = pl.ds(c, rows, stride=8) if rows > 1 else pl.ds(c, 1)
            put_rows(fall, below, rounded(dot(parents, split[c])))
            put_rows(adj_fall, below, adj_spread[:, c * k : (c + 1) * k])
        rows *= 8
    fetch.wait(5, 6, 7, 8)
    potential[...] = dot(get_rows(fall, pl.ds(0, rows)).astype(BF16), to_v[...]) + near_pot[...]
    gradient[...] = dot(get_rows(adj_fall, pl.ds(0, rows)).astype(BF16), to_m[...], NT) + near_grad[...]


def near_far_call(far, near, dens, cot, recv_e, recv_o, to_m, to_v, far_w, near_w):
    rows = dens.shape[0]
    k = to_m.shape[1]
    padded = recv_e.shape[0] - 2 * HW
    slots = far.shape[0] + near.shape[0]
    operands = (far, near, recv_e, recv_o, dens, cot, near_w, to_m, to_v, far_w)
    shapes = list(operands)
    shapes[6] = jax.ShapeDtypeStruct((slots, 128, 128), BF16)
    return pl.pallas_call(
        near_far_kernel,
        out_shape=[jax.ShapeDtypeStruct((rows, 128), F32)] * 2,
        in_specs=anywhere(10),
        out_specs=in_vmem(2),
        scratch_shapes=held(*shapes)
        + [
            pltpu.VMEM((rows // TILE, TILE, 256), BF16),
            pltpu.VMEM((2 * HW, 256), BF16),
            pltpu.VMEM((padded, rows), F32),
            pltpu.VMEM((padded, 2 * HW), F32),
            pltpu.VMEM((rows, 128), F32),
            pltpu.VMEM((rows, slots * 128), BF16),
            pltpu.VMEM((rows, slots * 128), BF16),
            pltpu.VMEM((far.shape[0] * 128, k), BF16),
            pltpu.VMEM((slots * 128, 128), BF16),
        ],
        compiler_params=pltpu.CompilerParams(vmem_limit_bytes=64 << 20),
        cost_estimate=pl.CostEstimate(flops=20 * 10**9, bytes_accessed=5 << 20, transcendentals=0),
        name="near_far",
    )(*operands)


def climb_call(dens, cot, far, near, to_m, to_v, merge, split, count, rim_shape):
    k = to_m.shape[1]
    chain = pltpu.VMEM((k // 128, dens.shape[0], 128), F32)
    operands = (dens, cot, to_m, to_v, merge, split, far, near)
    return pl.pallas_call(
        climb_kernel,
        out_shape=[
            jax.ShapeDtypeStruct((count * ROWS, 128), F32),
            rim_shape,
            rim_shape,
            jax.ShapeDtypeStruct((8, k, k), BF16),
        ],
        in_specs=anywhere(8),
        out_specs=in_vmem(4),
        scratch_shapes=held(*operands) + [chain, chain, pltpu.VMEM((k // 128, 8 * k, 128), F32)],
        compiler_params=pltpu.CompilerParams(vmem_limit_bytes=64 << 20),
        name="climb",
    )(*operands)


def fall_call(gathered, coarse_list, merge, split, far_w, to_m, to_v, near_pot, near_grad):
    rows = near_pot.shape[0]
    chain = pltpu.VMEM((merge.shape[2] // 128, rows, 128), F32)
    operands = (gathered, coarse_list, far_w, merge, split, to_m, to_v, near_pot, near_grad)
    return pl.pallas_call(
        fall_kernel,
        out_shape=[jax.ShapeDtypeStruct((rows, 128), F32)] * 2,
        in_specs=anywhere(9),
        out_specs=in_vmem(2),
        scratch_shapes=held(*operands)[:-1] + [pltpu.SemaphoreType.DMA((10,)), chain, chain],
        compiler_params=pltpu.CompilerParams(vmem_limit_bytes=64 << 20),
        name="fall",
    )(*operands)


def per_device(
    densities, cotangents, far_list, near_list, coarse_list,
    to_moments, merge_moments, far_translate, local_split, to_values, near_blocks,
):
    rows = densities.shape[0]
    k = to_moments.shape[1]
    count = lax.axis_size(AXES)
    slots = far_list.shape[0] + near_list.shape[0]
    rim_shape = jax.ShapeDtypeStruct((2 * HW + -(-slots // 16) * 16, 128), BF16)
    row, far_rim, near_rim, split = climb_call(
        densities, cotangents, far_list, near_list, to_moments, to_values, merge_moments, local_split,
        count, rim_shape,
    )
    pairs = [(i, i + 1) for i in range(1, count - 1, 2)]
    recv_o = lax.ppermute(far_rim, AXES, pairs + [(b, a) for a, b in pairs])
    recv_e = lax.ppermute(near_rim, AXES, [(i, i ^ 1) for i in range(count)])
    gathered = lax.all_to_all(row, AXES, 0, 0, tiled=True)
    sums = near_far_call(
        far_list, near_list, densities, cotangents, recv_e, recv_o,
        to_moments, to_values, far_translate, near_blocks,
    )
    return fall_call(
        gathered, coarse_list, merge_moments, split, far_translate, to_moments, to_values, *sums,
    )


def solution(mesh):
    rows = P(AXES, None)
    lists = P(None, AXES)
    return jax.shard_map(
        per_device,
        mesh=mesh,
        in_specs=(rows, rows, lists, lists) + (P(),) * 7,
        out_specs=(rows, rows),
        check_vma=False,
    )
```
